32 devices in a mesh: space: 8 (over z, x), tm: 4 (over y, core).
Axes of the slice: x: 2, y: 2, z: 4, core: 2. Of those that a mesh axis runs over, the one named last changes fastest.
Arguments:
- snapshots: float32 [4608, 8192], P('tm', 'space'), as said below
- block_starts: int32 [32], P('tm'), may hold values from 0 to 4352, as said below
- owner: int32 [9], replicated, may hold values from 0 to 3, as said below
Outputs:
- modes: float32 [20, 32, 2, 8192], P('tm', None, None, 'space')
The draws below stay inside these ranges and needn't reach their ends.
Inputs may be any that keep to these rules, and one draw needn't show every extreme that they name: `block_starts`: block k lies inside the snapshots held by index k // 8 of tm: its start is that range's first snapshot plus an even offset of 0 to 896; within one range the starts rise with k by 112 or more, the range's first block starts at offset 0 and its last at 896. `owner`: one index of tm owns exactly 5 frequencies, every other index owns one or more and fewer than 5. `snapshots`: finite real values.
All inputs are finite; a program needn't handle non-finite values.
Results may differ from the reference program's by a relative error of at most 0.0003.
Values sent between devices are 32-bit elements; how exact they have to be, the bound alone decides.
A program may use at most 64 MiB of HBM per device.

```python
import jax
import jax.numpy as jnp
from jax import lax

NFFT = 256
NF = 9
BLK_DEV = 8
NB = 32
TSEG = 1152
TIME = 4608
NPTS = 8192
FCAP = 5
N_TM = 4


def draw_snapshots(key, part):
    key_scale, key_noise, key_time, key_space = jax.random.split(key, 4)
    places = jnp.arange(NPTS, dtype=jnp.float32)
    ramp = 1.0 + 2.0 * places / NPTS
    uniform_draw = jax.random.uniform(key_scale, (NPTS,), jnp.float32)
    scales = jnp.exp(uniform_draw * jnp.log(10.0)) * ramp
    noise = jnp.clip(jax.random.normal(key_noise, (TIME, NPTS), jnp.float32), -4.0, 4.0)
    strength = 240.0
    signal = jnp.clip(jax.random.normal(key_time, (TIME,), jnp.float32), -4.0, 4.0)
    shape_field = jnp.clip(jax.random.normal(key_space, (NPTS,), jnp.float32), -4.0, 4.0)
    values = scales[None, :] * (noise + strength * signal[:, None] * shape_field[None, :])
    return values.astype(jnp.float32)


def draw_block_starts(key, part):
    shard_total = NB // BLK_DEV
    least_gap = 112
    gap_total = BLK_DEV - 1
    slack_half = (TSEG - NFFT - least_gap * gap_total) // 2
    pool = slack_half + gap_total - 1
    shard_keys = jax.random.split(key, shard_total)

    def draw_shard(shard_key):
        cuts = jnp.sort(jax.random.permutation(shard_key, pool)[:gap_total - 1].astype(jnp.int32))
        bounds = jnp.concatenate([jnp.full((1,), -1, jnp.int32), cuts, jnp.full((1,), pool, jnp.int32)])
        extra = bounds[1:] - bounds[:-1] - 1
        gaps = least_gap + 2 * extra
        return jnp.concatenate([jnp.zeros((1,), jnp.int32), jnp.cumsum(gaps).astype(jnp.int32)])
    local_starts = jax.vmap(draw_shard)(shard_keys)
    shifts = TSEG * jnp.arange(shard_total, dtype=jnp.int32)
    return (local_starts + shifts[:, None]).reshape(-1).astype(jnp.int32)


def draw_owner(key, part):
    shard_total = NB // BLK_DEV
    key_busy, key_order, key_rest = jax.random.split(key, 3)
    busiest = jax.random.randint(key_busy, (), 0, shard_total, dtype=jnp.int32)
    freq_order = jax.random.permutation(key_order, NF)
    extra = NF - FCAP - (shard_total - 1)
    offsets = jnp.concatenate([jnp.zeros((FCAP,), jnp.int32), jnp.arange(1, shard_total, dtype=jnp.int32), jax.random.randint(key_rest, (extra,), 1, shard_total, dtype=jnp.int32)])
    devices = (busiest + offsets) % shard_total
    owners = jnp.zeros((NF,), jnp.int32).at[freq_order].set(devices)
    return owners.astype(jnp.int32)


def setup_inputs(seed: int = 0) -> dict:
    streams_of = jax.random.split(jax.random.key(seed), 4)
    snapshots = draw_snapshots(jax.random.fold_in(streams_of[3], 71), 0)
    block_starts = draw_block_starts(jax.random.fold_in(streams_of[3], 71), 0)
    owner = draw_owner(jax.random.fold_in(streams_of[3], 71), 0)
    return dict(snapshots=snapshots, block_starts=block_starts, owner=owner)


def dft_table():
    times = jnp.arange(NFFT, dtype=jnp.int32)
    freqs = jnp.arange(NF, dtype=jnp.int32)
    phase = freqs[:, None] * times[None, :] % NFFT
    angle = 2.0 * jnp.pi / NFFT * phase.astype(jnp.float32)
    window = 0.5 - 0.5 * jnp.cos(2.0 * jnp.pi / NFFT * times.astype(jnp.float32))
    table = jnp.stack([window * jnp.cos(angle), -window * jnp.sin(angle)], axis=1)
    return table.reshape(2 * NF, NFFT)

def orth_pass(matrix, rows_total):
    gram = jnp.dot(matrix, matrix.T, precision=lax.Precision.HIGHEST) / rows_total
    factor = jnp.linalg.cholesky(gram)
    identity = jnp.eye(matrix.shape[0], dtype=matrix.dtype)
    inverse = jax.scipy.linalg.solve_triangular(factor, identity, lower=True)
    return jnp.dot(inverse, matrix, precision=lax.Precision.HIGHEST)

def reference(snapshots, block_starts, owner):
    table = dft_table()
    rows_total = 2.0 * NPTS
    collected = []
    for block in range(NB):
        segment = lax.dynamic_slice_in_dim(snapshots, block_starts[block].astype(jnp.int32), NFFT, 0)
        spectrum = jnp.dot(table, segment, precision=lax.Precision.HIGHEST)
        collected.append(spectrum.reshape(NF, 2 * NPTS))
    spectra = jnp.stack(collected)
    freq_ids = jnp.arange(NF, dtype=jnp.int32)
    modes = jnp.zeros((N_TM * FCAP, NB, 2 * NPTS), jnp.float32)
    for freq in range(NF):
        matrix = spectra[:, freq]
        basis = orth_pass(orth_pass(matrix, rows_total), rows_total)
        same_before = (owner == owner[freq]) & (freq_ids < freq)
        rank_in = jnp.sum(same_before.astype(jnp.int32)).astype(jnp.int32)
        slot_of = (owner[freq].astype(jnp.int32) * FCAP + rank_in).astype(jnp.int32)
        modes = lax.dynamic_update_slice(modes, basis[None].astype(modes.dtype), (slot_of, jnp.int32(0), jnp.int32(0)))
    return modes.reshape(N_TM * FCAP, NB, 2, NPTS)
```

```python
import functools

import jax
import jax.numpy as jnp
import numpy as np
from jax import lax
from jax.experimental import pallas as pl
from jax.experimental.pallas import tpu as pltpu
from jax.sharding import PartitionSpec as P

NFFT = 256
NF = 9
FCAP = 5
ROWS = 2 * NF
QP = 256
F32 = jnp.float32
BF16 = jnp.bfloat16
MESH = pl.DeviceIdType.MESH


def dft_table():
    times = np.arange(NFFT)
    phase = (np.arange(NF)[:, None] * times[None, :]) % NFFT
    angle = 2.0 * np.pi / NFFT * phase
    window = 0.5 - 0.5 * np.cos(2.0 * np.pi / NFFT * times)
    table = np.stack([window * np.cos(angle), -window * np.sin(angle)], axis=1)
    return table.reshape(ROWS, NFFT).astype(np.float32)


def split3(x):
    a = x.astype(BF16)
    rest = x - a.astype(F32)
    b = rest.astype(BF16)
    c = (rest - b.astype(F32)).astype(BF16)
    return a, b, c


def split2(x):
    a = x.astype(BF16)
    return a, (x - a.astype(F32)).astype(BF16)


def mm(a, b):
    return jnp.dot(a, b, preferred_element_type=F32)


def mm_t(a, b):
    return lax.dot_general(a, b, (((1,), (1,)), ((), ())), preferred_element_type=F32)


def pack(square):
    n = square.shape[0] // 4
    return jnp.concatenate([square[n * i : n * i + n] for i in range(4)], axis=1)


def unpack(packed):
    n = packed.shape[1] // 4
    return jnp.concatenate([packed[:, n * i : n * i + n] for i in range(4)], axis=0)


def inverse_factor(gram, panel=8):
    n = gram.shape[0]
    row = lax.broadcasted_iota(jnp.int32, (n, n), 0)
    col = lax.broadcasted_iota(jnp.int32, (n, n), 1)
    eye = jnp.where(row == col, 1.0, 0.0).astype(F32)
    trace = jnp.sum(jnp.sum(gram * eye, axis=1, keepdims=True), axis=0, keepdims=True)
    gram = gram + jnp.where(trace == 0.0, 1.0, 0.0) * eye
    work = jnp.concatenate([eye, gram, jnp.zeros((n, 128 - 2 * n), F32)], axis=1)
    rows = lax.broadcasted_iota(jnp.int32, (n, 128), 0)
    diag = jnp.ones((n, 128), F32)
    for first in range(0, n, panel):
        cols = [
            jnp.broadcast_to(work[:, n + first + j : n + first + j + 1], (n, 128))
            for j in range(panel)
        ]
        for j in range(panel):
            k = first + j
            pivot = jnp.broadcast_to(cols[j][k : k + 1], (n, 128))
            diag = jnp.where(rows == k, pivot, diag)
            factor = jnp.where(rows > k, cols[j] / pivot, 0.0)
            work = work - factor * work[k : k + 1]
            for i in range(j + 1, panel):
                cols[i] = cols[i] - factor * cols[i][k : k + 1]
    return (work / jnp.sqrt(diag))[:, :n]


def kernel(
    tms, sps, starts_ref, owner_ref, tab_ref, snap_hbm, out_ref,
    snap, tallf, tall, spec, send, recv, xs, bs, gacc, packed, gbuf, pinv, ibuf, bd,
    snap_sem, a2a_send, a2a_recv, g_send, g_recv, i_send, i_recv,
):
    quarters, samples = snap.shape[0], snap.shape[1]
    blocks = starts_ref.shape[0]
    nb = blocks * tms
    rows_total = 2.0 * quarters * QP * sps
    me = lax.axis_index("tm")
    my = lax.axis_index("space")
    first_worker = sps // 4

    loads = [
        pltpu.make_async_copy(snap_hbm.at[:, pl.ds(q * QP, QP)], snap.at[q], snap_sem.at[q])
        for q in range(quarters)
    ]
    for load in loads:
        load.start()
    barrier = pltpu.get_barrier_semaphore()
    for r in range(1, tms):
        pl.semaphore_signal(barrier, inc=1, device_id={"tm": lax.rem(me + r, tms)}, device_id_type=MESH)
    for r in range(1, sps):
        pl.semaphore_signal(barrier, inc=1, device_id={"space": lax.rem(my + r, sps)}, device_id_type=MESH)

    wide = jnp.concatenate([tab_ref[...], jnp.zeros((ROWS, samples - NFFT), F32)], axis=1)
    for k in range(blocks):
        tallf[:, k, :] = pltpu.roll(wide, starts_ref[k] - me * samples, 1)
    tall[...] = jnp.concatenate(split3(tallf[...].reshape(ROWS * blocks, samples)), axis=0)

    owners = [owner_ref[f] for f in range(NF)]
    slot_of = []
    for f in range(NF):
        rank = jnp.int32(0)
        for g in range(f):
            rank = rank + jnp.where(owners[g] == owners[f], 1, 0)
        slot_of.append(owners[f] * FCAP + rank)
    freq_in = []
    for slot in range(tms * FCAP):
        freq = jnp.int32(NF)
        for f in range(NF):
            freq = jnp.where(slot_of[f] == slot, f, freq)
        freq_in.append(freq)
    spec[NF] = jnp.zeros(spec.shape[1:], F32)
    gacc[...] = jnp.zeros(gacc.shape, F32)
    bd[...] = jnp.zeros(bd.shape, F32)

    order = [2, 1, 3] if tms == 4 else list(range(1, tms))
    m = ROWS * blocks
    sends = {}
    for q in range(quarters):
        loads[q].wait()
        s1, s2, s3 = split3(snap[q])
        p1 = mm(tall[...], s1)
        p2 = mm(tall[: 2 * m], s2)
        p3 = mm(tall[:m], s3)
        spectrum = p1[:m] + ((p1[m : 2 * m] + p2[:m]) + ((p1[2 * m :] + p2[m:]) + p3))
        for f in range(NF):
            for c in range(2):
                at = (2 * f + c) * blocks
                spec[f, :, c * QP : (c + 1) * QP] = spectrum[at : at + blocks]
        for peer in range(tms):
            for s in range(FCAP):
                send[q, peer, s] = spec[freq_in[peer * FCAP + s]]
        recv[q, me] = send[q, me]
        if q == 0:
            pl.semaphore_wait(barrier, tms + sps - 2)
        for r in order:
            peer = lax.rem(me + r, tms)
            sends[q, r] = pltpu.make_async_remote_copy(
                src_ref=send.at[q, peer], dst_ref=recv.at[q, me],
                send_sem=a2a_send.at[q, r], recv_sem=a2a_recv.at[q, r],
                device_id={"tm": peer}, device_id_type=MESH,
            )
            sends[q, r].start()

    def reduce_and_factor(turn):
        for s in range(FCAP):
            sl = pl.ds(s * nb, nb)
            packed[turn, s] = pack(gacc[sl, sl])
        for s in range(FCAP):
            worker = first_worker + s

            @pl.when(my != worker)
            def _():
                pltpu.make_async_remote_copy(
                    src_ref=packed.at[turn, s], dst_ref=gbuf.at[turn, my],
                    send_sem=g_send.at[turn, s], recv_sem=g_recv.at[turn, my],
                    device_id={"space": worker}, device_id_type=MESH,
                ).start()

        @pl.when((my >= first_worker) & (my < first_worker + FCAP))
        def _():
            mine = my - first_worker
            gbuf[turn, my] = packed[turn, mine]
            for r in range(1, sps):
                source = lax.rem(my + r, sps)
                pltpu.make_async_remote_copy(
                    src_ref=packed.at[turn, 0], dst_ref=gbuf.at[turn, source],
                    send_sem=g_send.at[turn, 0], recv_sem=g_recv.at[turn, source],
                    device_id={"space": source}, device_id_type=MESH,
                ).wait_recv()
            total = gbuf[turn, 0]
            for source in range(1, sps):
                total = total + gbuf[turn, source]
            inverse = pack(inverse_factor(unpack(total) / rows_total))
            pinv[turn] = inverse
            ibuf[turn, mine] = inverse
            copies = []
            for r in range(1, sps):
                peer = lax.rem(my + r, sps)
                copies.append(
                    pltpu.make_async_remote_copy(
                        src_ref=pinv.at[turn], dst_ref=ibuf.at[turn, mine],
                        send_sem=i_send.at[turn, r], recv_sem=i_recv.at[turn, mine],
                        device_id={"space": peer}, device_id_type=MESH,
                    )
                )
                copies[-1].start()
            for copy in copies:
                copy.wait_send()

        for s in range(FCAP):
            worker = first_worker + s

            @pl.when(my != worker)
            def _():
                pltpu.make_async_remote_copy(
                    src_ref=packed.at[turn, s], dst_ref=ibuf.at[turn, s],
                    send_sem=g_send.at[turn, s], recv_sem=i_recv.at[turn, s],
                    device_id={"space": worker}, device_id_type=MESH,
                ).wait()

            bd[s * nb : (s + 1) * nb, s * nb : (s + 1) * nb] = unpack(ibuf[turn, s])

    size = FCAP * nb
    for q in range(quarters):
        for r in order:
            sends[q, r].wait_recv()
        stacked = jnp.concatenate(
            [recv[q, :, s].reshape(nb, 2 * QP) for s in range(FCAP)], axis=0
        )
        x1, x2, x3 = split3(stacked)
        xs[q, 0], xs[q, 1], xs[q, 2] = x1, x2, x3
        p1 = mm_t(xs[q].reshape(3 * size, 2 * QP), x1)
        p2 = mm_t(xs[q, :2].reshape(2 * size, 2 * QP), x2)
        p3 = mm_t(x1, x3)
        gacc[...] += p1[:size] + (
            (p1[size : 2 * size] + p2[:size]) + ((p1[2 * size :] + p2[size:]) + p3)
        )
    reduce_and_factor(0)

    d1, d2, d3 = split3(bd[...])
    d321 = jnp.concatenate([d1, d2, d3], axis=0)
    gacc[...] = jnp.zeros(gacc.shape, F32)
    for q in range(quarters):
        p1 = mm(d321, xs[q, 0])
        p2 = mm(d321[: 2 * size], xs[q, 1])
        p3 = mm(d1, xs[q, 2])
        basis = p1[:size] + (
            (p1[size : 2 * size] + p2[:size]) + ((p1[2 * size :] + p2[size:]) + p3)
        )
        b1, b2 = split2(basis)
        bs[q, 0], bs[q, 1] = b1, b2
        p1 = mm_t(bs[q].reshape(2 * size, 2 * QP), b1)
        gacc[...] += p1[:size] + (p1[size:] + mm_t(b1, b2))
    reduce_and_factor(1)

    d1, d2 = split2(bd[...])
    d21 = jnp.concatenate([d1, d2], axis=0)
    for q in range(quarters):
        p1 = mm(d21, bs[q, 0])
        out_ref[q] = p1[:size] + (p1[size:] + mm(d1, bs[q, 1]))
    for q in range(quarters):
        for r in order:
            sends[q, r].wait_send()


def local(tms, sps, snapshots, block_starts, owner):
    samples, points = snapshots.shape
    blocks = block_starts.shape[0]
    nb = blocks * tms
    size = FCAP * nb
    quarters = points // QP
    table = jnp.asarray(dft_table())
    vm = pltpu.VMEM
    dma = pltpu.SemaphoreType.DMA
    out = pl.pallas_call(
        functools.partial(kernel, tms, sps),
        out_shape=jax.ShapeDtypeStruct((quarters, size, 2 * QP), F32),
        in_specs=[
            pl.BlockSpec(memory_space=pltpu.SMEM),
            pl.BlockSpec(memory_space=pltpu.SMEM),
            pl.BlockSpec(memory_space=pltpu.VMEM),
            pl.BlockSpec(memory_space=pl.ANY),
        ],
        out_specs=pl.BlockSpec(memory_space=pltpu.VMEM),
        scratch_shapes=[
            vm((quarters, samples, QP), F32),
            vm((ROWS, blocks, samples), F32),
            vm((3 * ROWS * blocks, samples), BF16),
            vm((NF + 1, blocks, 2 * QP), F32),
            vm((quarters, tms, FCAP, blocks, 2 * QP), F32),
            vm((quarters, tms, FCAP, blocks, 2 * QP), F32),
            vm((quarters, 3, size, 2 * QP), BF16),
            vm((quarters, 2, size, 2 * QP), BF16),
            vm((size, size), F32),
            vm((2, FCAP, nb // 4, nb * 4), F32),
            vm((2, sps, nb // 4, nb * 4), F32),
            vm((2, nb // 4, nb * 4), F32),
            vm((2, FCAP, nb // 4, nb * 4), F32),
            vm((size, size), F32),
            dma((quarters,)),
            dma((quarters, tms)),
            dma((quarters, tms)),
            dma((2, FCAP)),
            dma((2, sps)),
            dma((2, sps)),
            dma((2, FCAP)),
        ],
        compiler_params=pltpu.CompilerParams(
            collective_id=0, has_side_effects=True, vmem_limit_bytes=48 * 1024 * 1024
        ),
    )(block_starts, owner, table, snapshots)
    out = out.reshape(quarters, FCAP, nb, 2, QP).transpose(1, 2, 3, 0, 4)
    return out.reshape(FCAP, nb, 2, points)


def solution(mesh):
    placed = (P("tm", "space"), P("tm"), P())
    return jax.shard_map(
        functools.partial(local, mesh.shape["tm"], mesh.shape["space"]),
        mesh=mesh, in_specs=placed, out_specs=P("tm", None, None, "space"), check_vma=False,
    )
```

```python
import functools

import jax
import jax.numpy as jnp
import numpy as np
from jax import lax
from jax.experimental import pallas as pl
from jax.experimental.pallas import tpu as pltpu
from jax.sharding import PartitionSpec as P

NFFT = 256
NF = 9
FCAP = 5
PAIR_CAP = 7
ROWS = 2 * NF
QP = 256
F32 = jnp.float32
BF16 = jnp.bfloat16
MESH = pl.DeviceIdType.MESH


def dft_table():
    times = np.arange(NFFT)
    phase = (np.arange(NF)[:, None] * times[None, :]) % NFFT
    angle = 2.0 * np.pi / NFFT * phase
    window = 0.5 - 0.5 * np.cos(2.0 * np.pi / NFFT * times)
    table = np.stack([window * np.cos(angle), -window * np.sin(angle)], axis=1)
    return table.reshape(ROWS, NFFT).astype(np.float32)


def split3(x):
    a = x.astype(BF16)
    rest = x - a.astype(F32)
    b = rest.astype(BF16)
    c = (rest - b.astype(F32)).astype(BF16)
    return a, b, c


def split2(x):
    a = x.astype(BF16)
    return a, (x - a.astype(F32)).astype(BF16)


def mm(a, b):
    return jnp.dot(a, b, preferred_element_type=F32)


def mm_t(a, b):
    return lax.dot_general(a, b, (((1,), (1,)), ((), ())), preferred_element_type=F32)


def pack(square):
    n = square.shape[0] // 4
    return jnp.concatenate([square[n * i : n * i + n] for i in range(4)], axis=1)


def unpack(packed):
    n = packed.shape[1] // 4
    return jnp.concatenate([packed[:, n * i : n * i + n] for i in range(4)], axis=0)


def inverse_factor(gram, panel=8):
    n = gram.shape[0]
    row = lax.broadcasted_iota(jnp.int32, (n, n), 0)
    col = lax.broadcasted_iota(jnp.int32, (n, n), 1)
    eye = jnp.where(row == col, 1.0, 0.0).astype(F32)
    trace = jnp.sum(jnp.sum(gram * eye, axis=1, keepdims=True), axis=0, keepdims=True)
    gram = gram + jnp.where(trace == 0.0, 1.0, 0.0) * eye
    work = jnp.concatenate([eye, gram, jnp.zeros((n, 128 - 2 * n), F32)], axis=1)
    rows = lax.broadcasted_iota(jnp.int32, (n, 128), 0)
    diag = jnp.ones((n, 128), F32)
    for first in range(0, n, panel):
        cols = [
            jnp.broadcast_to(work[:, n + first + j : n + first + j + 1], (n, 128))
            for j in range(panel)
        ]
        for j in range(panel):
            k = first + j
            pivot = jnp.broadcast_to(cols[j][k : k + 1], (n, 128))
            diag = jnp.where(rows == k, pivot, diag)
            factor = jnp.where(rows > k, cols[j] / pivot, 0.0)
            work = work - factor * work[k : k + 1]
            for i in range(j + 1, panel):
                cols[i] = cols[i] - factor * cols[i][k : k + 1]
    return (work / jnp.sqrt(diag))[:, :n]


def kernel(
    tms, sps, starts_hbm, owner_hbm, tab_hbm, snap_hbm, out_ref,
    starts_ref, owner_ref, tab_ref, snap, tallf, tall, spec, near, far, sib_in, xbuf,
    xs, bs, gacc, packed, gbuf, pinv, ibuf, bd,
    in_sem, snap_sem, a2a_send, a2a_recv, g_send, g_recv, i_send, i_recv, *far_in,
):
    quarters, samples = snap.shape[0], snap.shape[1]
    blocks = starts_hbm.shape[0]
    nb = blocks * tms
    rows_total = 2.0 * quarters * QP * sps
    me = lax.axis_index("tm")
    my = lax.axis_index("space")
    first_worker = sps // 4
    pair, half = me // 2, me % 2
    sibling = 2 * pair + (1 - half)
    across = 2 * (1 - pair) + half
    across_sibling = 2 * (1 - pair) + (1 - half)

    small = [
        pltpu.make_async_copy(source, target, in_sem.at[i])
        for i, (source, target) in enumerate(
            [(starts_hbm, starts_ref), (owner_hbm, owner_ref), (tab_hbm, tab_ref)]
        )
    ]
    for load in small:
        load.start()
    loads = [
        pltpu.make_async_copy(snap_hbm.at[:, pl.ds(q * QP, QP)], snap.at[q], snap_sem.at[q])
        for q in range(quarters)
    ]
    for load in loads:
        load.start()
    barrier = pltpu.get_barrier_semaphore()
    for peer in (sibling, across):
        pl.semaphore_signal(barrier, inc=1, device_id={"tm": peer}, device_id_type=MESH)
    for r in range(1, sps):
        pl.semaphore_signal(barrier, inc=1, device_id={"space": lax.rem(my + r, sps)}, device_id_type=MESH)
    for load in small:
        load.wait()

    wide = jnp.concatenate([tab_ref[...], jnp.zeros((ROWS, samples - NFFT), F32)], axis=1)
    for k in range(blocks):
        tallf[:, k, :] = pltpu.roll(wide, starts_ref[k] - me * samples, 1)
    tall[...] = jnp.concatenate(split3(tallf[...].reshape(ROWS * blocks, samples)), axis=0)

    owners = [owner_ref[f] for f in range(NF)]
    owner_pair = [jnp.where(owners[f] >= 2, 1, 0) for f in range(NF)]
    rank, pair_rank = [], []
    for f in range(NF):
        rank.append(sum([jnp.where(owners[g] == owners[f], 1, 0) for g in range(f)], jnp.int32(0)))
        pair_rank.append(
            sum([jnp.where(owner_pair[g] == owner_pair[f], 1, 0) for g in range(f)], jnp.int32(0))
        )

    def owned(holder, s):
        freq, place = jnp.int32(NF), jnp.int32(0)
        for f in range(NF):
            hit = (owners[f] == holder) & (rank[f] == s)
            freq = jnp.where(hit, f, freq)
            place = jnp.where(hit, pair_rank[f], place)
        return freq, place

    mine = [owned(me, s) for s in range(FCAP)]
    theirs = [owned(sibling, s)[0] for s in range(FCAP)]
    distant = []
    for place in range(PAIR_CAP):
        freq = jnp.int32(NF)
        for f in range(NF):
            freq = jnp.where((owner_pair[f] == 1 - pair) & (pair_rank[f] == place), f, freq)
        distant.append(freq)
    spec[NF] = jnp.zeros(spec.shape[1:], F32)
    gacc[...] = jnp.zeros(gacc.shape, F32)
    bd[...] = jnp.zeros(bd.shape, F32)

    def hop(source, target, kind, q, peer):
        return pltpu.make_async_remote_copy(
            src_ref=source, dst_ref=target,
            send_sem=a2a_send.at[q, kind], recv_sem=a2a_recv.at[q, kind],
            device_id={"tm": peer}, device_id_type=MESH,
        )

    across_hops = [hop(far.at[q], far_in[q].at[0], 0, q, across) for q in range(quarters)]
    sibling_hops = [hop(near.at[q, 1], sib_in.at[q], 1, q, sibling) for q in range(quarters)]
    relays = [hop(far_in[q].at[0], far_in[q].at[1], 2, q, sibling) for q in range(quarters)]
    m = ROWS * blocks
    for q in range(quarters):
        loads[q].wait()
        s1, s2, s3 = split3(snap[q])
        p1 = mm(tall[...], s1)
        p2 = mm(tall[: 2 * m], s2)
        p3 = mm(tall[:m], s3)
        spectrum = p1[:m] + ((p1[m : 2 * m] + p2[:m]) + ((p1[2 * m :] + p2[m:]) + p3))
        for f in range(NF):
            for c in range(2):
                at = (2 * f + c) * blocks
                spec[f, :, c * QP : (c + 1) * QP] = spectrum[at : at + blocks]
        for place in range(PAIR_CAP):
            far[q, place] = spec[distant[place]]
        if q == 0:
            pl.semaphore_wait(barrier, sps + 1)
        across_hops[q].start()
        for s in range(FCAP):
            near[q, 0, s] = spec[mine[s][0]]
            near[q, 1, s] = spec[theirs[s]]
        sibling_hops[q].start()

    def reduce_and_factor(turn):
        for s in range(FCAP):
            sl = pl.ds(s * nb, nb)
            packed[turn, s] = pack(gacc[sl, sl])
        for s in range(FCAP):
            worker = first_worker + s

            @pl.when(my != worker)
            def _():
                pltpu.make_async_remote_copy(
                    src_ref=packed.at[turn, s], dst_ref=gbuf.at[turn, my],
                    send_sem=g_send.at[turn, s], recv_sem=g_recv.at[turn, my],
                    device_id={"space": worker}, device_id_type=MESH,
                ).start()

        @pl.when((my >= first_worker) & (my < first_worker + FCAP))
        def _():
            mine = my - first_worker
            gbuf[turn, my] = packed[turn, mine]
            for r in range(1, sps):
                source = lax.rem(my + r, sps)
                pltpu.make_async_remote_copy(
                    src_ref=packed.at[turn, 0], dst_ref=gbuf.at[turn, source],
                    send_sem=g_send.at[turn, 0], recv_sem=g_recv.at[turn, source],
                    device_id={"space": source}, device_id_type=MESH,
                ).wait_recv()
            total = gbuf[turn, 0]
            for source in range(1, sps):
                total = total + gbuf[turn, source]
            inverse = pack(inverse_factor(unpack(total) / rows_total))
            pinv[turn] = inverse
            ibuf[turn, mine] = inverse
            copies = []
            for r in range(1, sps):
                peer = lax.rem(my + r, sps)
                copies.append(
                    pltpu.make_async_remote_copy(
                        src_ref=pinv.at[turn], dst_ref=ibuf.at[turn, mine],
                        send_sem=i_send.at[turn, r], recv_sem=i_recv.at[turn, mine],
                        device_id={"space": peer}, device_id_type=MESH,
                    )
                )
                copies[-1].start()
            for copy in copies:
                copy.wait_send()

        for s in range(FCAP):
            worker = first_worker + s

            @pl.when(my != worker)
            def _():
                pltpu.make_async_remote_copy(
                    src_ref=packed.at[turn, s], dst_ref=ibuf.at[turn, s],
                    send_sem=g_send.at[turn, s], recv_sem=i_recv.at[turn, s],
                    device_id={"space": worker}, device_id_type=MESH,
                ).wait()

            bd[s * nb : (s + 1) * nb, s * nb : (s + 1) * nb] = unpack(ibuf[turn, s])

    size = FCAP * nb
    across_hops[0].wait_recv()
    relays[0].start()
    for q in range(quarters):
        if q + 1 < quarters:
            across_hops[q + 1].wait_recv()
            relays[q + 1].start()
        sibling_hops[q].wait_recv()
        relays[q].wait_recv()
        xbuf[me] = near[q, 0]
        xbuf[sibling] = sib_in[q]
        for s in range(FCAP):
            freq, place = mine[s]
            xbuf[across, s] = jnp.where(freq < NF, far_in[q][0, place], 0.0)
            xbuf[across_sibling, s] = jnp.where(freq < NF, far_in[q][1, place], 0.0)
        stacked = jnp.concatenate(
            [xbuf[:, s].reshape(nb, 2 * QP) for s in range(FCAP)], axis=0
        )
        x1, x2, x3 = split3(stacked)
        xs[q, 0], xs[q, 1], xs[q, 2] = x1, x2, x3
        p1 = mm_t(xs[q].reshape(3 * size, 2 * QP), x1)
        p2 = mm_t(xs[q, :2].reshape(2 * size, 2 * QP), x2)
        p3 = mm_t(x1, x3)
        gacc[...] += p1[:size] + (
            (p1[size : 2 * size] + p2[:size]) + ((p1[2 * size :] + p2[size:]) + p3)
        )
    reduce_and_factor(0)

    d1, d2, d3 = split3(bd[...])
    d321 = jnp.concatenate([d1, d2, d3], axis=0)
    gacc[...] = jnp.zeros(gacc.shape, F32)
    for q in range(quarters):
        p1 = mm(d321, xs[q, 0])
        p2 = mm(d321[: 2 * size], xs[q, 1])
        p3 = mm(d1, xs[q, 2])
        basis = p1[:size] + (
            (p1[size : 2 * size] + p2[:size]) + ((p1[2 * size :] + p2[size:]) + p3)
        )
        b1, b2 = split2(basis)
        bs[q, 0], bs[q, 1] = b1, b2
        p1 = mm_t(bs[q].reshape(2 * size, 2 * QP), b1)
        gacc[...] += p1[:size] + (p1[size:] + mm_t(b1, b2))
    reduce_and_factor(1)

    d1, d2 = split2(bd[...])
    d21 = jnp.concatenate([d1, d2], axis=0)
    for q in range(quarters):
        p1 = mm(d21, bs[q, 0])
        modes = p1[:size] + (p1[size:] + mm(d1, bs[q, 1]))
        for s in range(FCAP):
            for c in range(2):
                part = modes[s * nb : (s + 1) * nb, c * QP : (c + 1) * QP]
                out_ref[s, :, c, q * QP : (q + 1) * QP] = part
    for q in range(quarters):
        for copy in (across_hops[q], sibling_hops[q], relays[q]):
            copy.wait_send()


def local(tms, sps, snapshots, block_starts, owner):
    samples, points = snapshots.shape
    blocks = block_starts.shape[0]
    nb = blocks * tms
    size = FCAP * nb
    quarters = points // QP
    table = jnp.asarray(dft_table())
    vm = pltpu.VMEM
    dma = pltpu.SemaphoreType.DMA
    return pl.pallas_call(
        functools.partial(kernel, tms, sps),
        out_shape=jax.ShapeDtypeStruct((FCAP, nb, 2, points), F32),
        in_specs=[pl.BlockSpec(memory_space=pltpu.HBM)] * 4,
        out_specs=pl.BlockSpec(memory_space=pltpu.VMEM),
        scratch_shapes=[
            pltpu.SMEM((blocks,), jnp.int32),
            pltpu.SMEM((NF,), jnp.int32),
            vm((ROWS, NFFT), F32),
            vm((quarters, samples, QP), F32),
            vm((ROWS, blocks, samples), F32),
            vm((3 * ROWS * blocks, samples), BF16),
            vm((NF + 1, blocks, 2 * QP), F32),
            vm((quarters, 2, FCAP, blocks, 2 * QP), F32),
            vm((quarters, PAIR_CAP, blocks, 2 * QP), F32),
            vm((quarters, FCAP, blocks, 2 * QP), F32),
            vm((tms, FCAP, blocks, 2 * QP), F32),
            vm((quarters, 3, size, 2 * QP), BF16),
            vm((quarters, 2, size, 2 * QP), BF16),
            vm((size, size), F32),
            vm((2, FCAP, nb // 4, nb * 4), F32),
            vm((2, sps, nb // 4, nb * 4), F32),
            vm((2, nb // 4, nb * 4), F32),
            vm((2, FCAP, nb // 4, nb * 4), F32),
            vm((size, size), F32),
            dma((3,)),
            dma((quarters,)),
            dma((quarters, 3)),
            dma((quarters, 3)),
            dma((2, FCAP)),
            dma((2, sps)),
            dma((2, sps)),
            dma((2, FCAP)),
            *[vm((2, PAIR_CAP, blocks, 2 * QP), F32) for _ in range(quarters)],
        ],
        compiler_params=pltpu.CompilerParams(
            collective_id=0, has_side_effects=True, vmem_limit_bytes=64 * 1024 * 1024 - 65536
        ),
    )(block_starts, owner, table, snapshots)


def solution(mesh):
    placed = (P("tm", "space"), P("tm"), P())
    return jax.shard_map(
        functools.partial(local, mesh.shape["tm"], mesh.shape["space"]),
        mesh=mesh, in_specs=placed, out_specs=P("tm", None, None, "space"), check_vma=False,
    )
```

```python
import functools

import jax
import jax.numpy as jnp
import numpy as np
from jax import lax
from jax.experimental import pallas as pl
from jax.experimental.pallas import tpu as pltpu
from jax.sharding import PartitionSpec as P

NFFT = 256
NF = 9
FCAP = 5
PAIR_CAP = 7
GAP = 112
VMEM_BYTES = 64 * 1024 * 1024 - 65536
ROWS = 2 * NF
QP = 256
F32 = jnp.float32
BF16 = jnp.bfloat16
MESH = pl.DeviceIdType.MESH


def dft_table():
    times = np.arange(NFFT)
    phase = (np.arange(NF)[:, None] * times[None, :]) % NFFT
    angle = 2.0 * np.pi / NFFT * phase
    window = 0.5 - 0.5 * np.cos(2.0 * np.pi / NFFT * times)
    table = np.stack([window * np.cos(angle), -window * np.sin(angle)], axis=1)
    return table.reshape(ROWS, NFFT).astype(np.float32)


def split3(x):
    a = x.astype(BF16)
    rest = x - a.astype(F32)
    b = rest.astype(BF16)
    c = (rest - b.astype(F32)).astype(BF16)
    return a, b, c


def split2(x):
    a = x.astype(BF16)
    return a, (x - a.astype(F32)).astype(BF16)


def mm(a, b):
    return jnp.dot(a, b, preferred_element_type=F32)


def mm_t(a, b):
    return lax.dot_general(a, b, (((1,), (1,)), ((), ())), preferred_element_type=F32)


def pack(square):
    n = square.shape[0] // 4
    return jnp.concatenate([square[n * i : n * i + n] for i in range(4)], axis=1)


def unpack(packed):
    n = packed.shape[1] // 4
    return jnp.concatenate([packed[:, n * i : n * i + n] for i in range(4)], axis=0)


def inverse_factor(gram, panel=8):
    n = gram.shape[0]
    row = lax.broadcasted_iota(jnp.int32, (n, n), 0)
    col = lax.broadcasted_iota(jnp.int32, (n, n), 1)
    eye = jnp.where(row == col, 1.0, 0.0).astype(F32)
    trace = jnp.sum(jnp.sum(gram * eye, axis=1, keepdims=True), axis=0, keepdims=True)
    gram = gram + jnp.where(trace == 0.0, 1.0, 0.0) * eye
    work = jnp.concatenate([eye, gram, jnp.zeros((n, 128 - 2 * n), F32)], axis=1)
    rows = lax.broadcasted_iota(jnp.int32, (n, 128), 0)
    diag = jnp.ones((n, 128), F32)
    for first in range(0, n, panel):
        cols = [
            jnp.broadcast_to(work[:, n + first + j : n + first + j + 1], (n, 128))
            for j in range(panel)
        ]
        for j in range(panel):
            k = first + j
            pivot = jnp.broadcast_to(cols[j][k : k + 1], (n, 128))
            diag = jnp.where(rows == k, pivot, diag)
            factor = jnp.where(rows > k, cols[j] * (1.0 / cols[j][k : k + 1]), 0.0)
            work = work - factor * work[k : k + 1]
            for i in range(j + 1, panel):
                cols[i] = cols[i] - factor * cols[i][k : k + 1]
    return (work / jnp.sqrt(diag))[:, :n]


def kernel(
    tms, sps, starts_hbm, owner_hbm, tab_hbm, snap_hbm, basis_out, factor_out,
    starts_ref, owner_ref, tab_ref, snap, tallf, tall, spec, near, far, sib_in, xbuf,
    xs, bs, gacc, packed, gbuf, pinv, ibuf, bd,
    in_sem, snap_sem, a2a_send, a2a_recv, g_send, g_recv, i_send, i_recv, *far_in,
):
    quarters, samples = snap.shape[0], snap.shape[1]
    blocks = starts_hbm.shape[0]
    nb = blocks * tms
    rows_total = 2.0 * quarters * QP * sps
    me = lax.axis_index("tm")
    my = lax.axis_index("space")
    first_worker = sps // 4
    pair, half = me // 2, me % 2
    sibling = 2 * pair + (1 - half)
    across = 2 * (1 - pair) + half
    across_sibling = 2 * (1 - pair) + (1 - half)

    small = [
        pltpu.make_async_copy(source, target, in_sem.at[i])
        for i, (source, target) in enumerate(
            [(starts_hbm, starts_ref), (owner_hbm, owner_ref), (tab_hbm, tab_ref)]
        )
    ]
    for load in small:
        load.start()
    loads = [
        pltpu.make_async_copy(snap_hbm.at[:, pl.ds(q * QP, QP)], snap.at[q], snap_sem.at[q])
        for q in range(quarters)
    ]
    for load in loads:
        load.start()
    barrier = pltpu.get_barrier_semaphore()
    for peer in (sibling, across):
        pl.semaphore_signal(barrier, inc=1, device_id={"tm": peer}, device_id_type=MESH)
    for r in range(1, sps):
        pl.semaphore_signal(barrier, inc=1, device_id={"space": lax.rem(my + r, sps)}, device_id_type=MESH)
    tallf[...] = jnp.zeros(tallf.shape, F32)
    for load in small:
        load.wait()

    span = 2 * NFFT
    wide = jnp.concatenate([tab_ref[...], jnp.zeros((ROWS, span - NFFT), F32)], axis=1)
    for k in range(blocks):
        base = k * GAP // 128 * 128
        keep = min(span, samples - base)
        moved = pltpu.roll(wide, starts_ref[k] - me * samples - base, 1)
        tallf[:, k, base : base + keep] = moved[:, :keep]
    tall[...] = jnp.concatenate(split3(tallf[...].reshape(ROWS * blocks, samples)), axis=0)

    owners = [owner_ref[f] for f in range(NF)]
    owner_pair = [jnp.where(owners[f] >= 2, 1, 0) for f in range(NF)]
    rank, pair_rank = [], []
    for f in range(NF):
        rank.append(sum([jnp.where(owners[g] == owners[f], 1, 0) for g in range(f)], jnp.int32(0)))
        pair_rank.append(
            sum([jnp.where(owner_pair[g] == owner_pair[f], 1, 0) for g in range(f)], jnp.int32(0))
        )

    def owned(holder, s):
        freq, place = jnp.int32(NF), jnp.int32(0)
        for f in range(NF):
            hit = (owners[f] == holder) & (rank[f] == s)
            freq = jnp.where(hit, f, freq)
            place = jnp.where(hit, pair_rank[f], place)
        return freq, place

    mine = [owned(me, s) for s in range(FCAP)]
    theirs = [owned(sibling, s)[0] for s in range(FCAP)]
    distant = []
    for place in range(PAIR_CAP):
        freq = jnp.int32(NF)
        for f in range(NF):
            freq = jnp.where((owner_pair[f] == 1 - pair) & (pair_rank[f] == place), f, freq)
        distant.append(freq)
    spec[NF] = jnp.zeros(spec.shape[1:], F32)
    gacc[...] = jnp.zeros(gacc.shape, F32)
    bd[...] = jnp.zeros(bd.shape, F32)

    def hop(source, target, kind, q, peer):
        return pltpu.make_async_remote_copy(
            src_ref=source, dst_ref=target,
            send_sem=a2a_send.at[q, kind], recv_sem=a2a_recv.at[q, kind],
            device_id={"tm": peer}, device_id_type=MESH,
        )

    across_hops = [hop(far.at[q], far_in[q].at[0], 0, q, across) for q in range(quarters)]
    sibling_hops = [hop(near.at[q, 1], sib_in.at[q], 1, q, sibling) for q in range(quarters)]
    relays = [hop(far_in[q].at[0], far_in[q].at[1], 2, q, sibling) for q in range(quarters)]
    m = ROWS * blocks
    for q in range(quarters):
        loads[q].wait()
        s1, s2, s3 = split3(snap[q])
        p1 = mm(tall[...], s1)
        p2 = mm(tall[: 2 * m], s2)
        p3 = mm(tall[:m], s3)
        spectrum = p1[:m] + ((p1[m : 2 * m] + p2[:m]) + ((p1[2 * m :] + p2[m:]) + p3))
        for f in range(NF):
            for c in range(2):
                at = (2 * f + c) * blocks
                spec[f, :, c * QP : (c + 1) * QP] = spectrum[at : at + blocks]
        for place in range(PAIR_CAP):
            far[q, place] = spec[distant[place]]
        if q == 0:
            pl.semaphore_wait(barrier, sps + 1)
        across_hops[q].start()
        for s in range(FCAP):
            near[q, 0, s] = spec[mine[s][0]]
            near[q, 1, s] = spec[theirs[s]]
        sibling_hops[q].start()

    def reduce_and_factor(turn):
        for s in range(FCAP):
            sl = pl.ds(s * nb, nb)
            packed[turn, s] = pack(gacc[sl, sl])
        for s in range(FCAP):
            worker = first_worker + s

            @pl.when(my != worker)
            def _():
                pltpu.make_async_remote_copy(
                    src_ref=packed.at[turn, s], dst_ref=gbuf.at[turn, my],
                    send_sem=g_send.at[turn, s], recv_sem=g_recv.at[turn, my],
                    device_id={"space": worker}, device_id_type=MESH,
                ).start()

        @pl.when((my >= first_worker) & (my < first_worker + FCAP))
        def _():
            mine = my - first_worker
            gbuf[turn, my] = packed[turn, mine]
            for r in range(1, sps):
                source = lax.rem(my + r, sps)
                pltpu.make_async_remote_copy(
                    src_ref=packed.at[turn, 0], dst_ref=gbuf.at[turn, source],
                    send_sem=g_send.at[turn, 0], recv_sem=g_recv.at[turn, source],
                    device_id={"space": source}, device_id_type=MESH,
                ).wait_recv()
            total = gbuf[turn, 0]
            for source in range(1, sps):
                total = total + gbuf[turn, source]
            inverse = pack(inverse_factor(unpack(total) / rows_total))
            pinv[turn] = inverse
            ibuf[turn, mine] = inverse
            copies = []
            for r in range(1, sps):
                peer = lax.rem(my + r, sps)
                copies.append(
                    pltpu.make_async_remote_copy(
                        src_ref=pinv.at[turn], dst_ref=ibuf.at[turn, mine],
                        send_sem=i_send.at[turn, r], recv_sem=i_recv.at[turn, mine],
                        device_id={"space": peer}, device_id_type=MESH,
                    )
                )
                copies[-1].start()
            for copy in copies:
                copy.wait_send()

        for s in range(FCAP):
            worker = first_worker + s

            @pl.when(my != worker)
            def _():
                pltpu.make_async_remote_copy(
                    src_ref=packed.at[turn, s], dst_ref=ibuf.at[turn, s],
                    send_sem=g_send.at[turn, s], recv_sem=i_recv.at[turn, s],
                    device_id={"space": worker}, device_id_type=MESH,
                ).wait()

            if turn == 0:
                bd[s * nb : (s + 1) * nb, s * nb : (s + 1) * nb] = unpack(ibuf[turn, s])
            else:
                factor_out[s] = ibuf[turn, s]

    size = FCAP * nb
    across_hops[0].wait_recv()
    relays[0].start()
    for q in range(quarters):
        if q + 1 < quarters:
            across_hops[q + 1].wait_recv()
            relays[q + 1].start()
        sibling_hops[q].wait_recv()
        relays[q].wait_recv()
        xbuf[me] = near[q, 0]
        xbuf[sibling] = sib_in[q]
        for s in range(FCAP):
            freq, place = mine[s]
            xbuf[across, s] = jnp.where(freq < NF, far_in[q][0, place], 0.0)
            xbuf[across_sibling, s] = jnp.where(freq < NF, far_in[q][1, place], 0.0)
        stacked = jnp.concatenate(
            [xbuf[:, s].reshape(nb, 2 * QP) for s in range(FCAP)], axis=0
        )
        x1, x2, x3 = split3(stacked)
        xs[q, 0], xs[q, 1], xs[q, 2] = x1, x2, x3
        p1 = mm_t(xs[q].reshape(3 * size, 2 * QP), x1)
        p2 = mm_t(xs[q, :2].reshape(2 * size, 2 * QP), x2)
        p3 = mm_t(x1, x3)
        gacc[...] += p1[:size] + (
            (p1[size : 2 * size] + p2[:size]) + ((p1[2 * size :] + p2[size:]) + p3)
        )
    reduce_and_factor(0)

    d1, d2, d3 = split3(bd[...])
    d321 = jnp.concatenate([d1, d2, d3], axis=0)
    gacc[...] = jnp.zeros(gacc.shape, F32)
    stores = [
        pltpu.make_async_copy(bs.at[q], basis_out.at[q], snap_sem.at[q]) for q in range(quarters)
    ]
    for q in range(quarters):
        p1 = mm(d321, xs[q, 0])
        p2 = mm(d321[: 2 * size], xs[q, 1])
        p3 = mm(d1, xs[q, 2])
        basis = p1[:size] + (
            (p1[size : 2 * size] + p2[:size]) + ((p1[2 * size :] + p2[size:]) + p3)
        )
        b1, b2 = split2(basis)
        bs[q, 0], bs[q, 1] = b1, b2
        stores[q].start()
        p1 = mm_t(bs[q].reshape(2 * size, 2 * QP), b1)
        gacc[...] += p1[:size] + (p1[size:] + mm_t(b1, b2))
    reduce_and_factor(1)

    for store in stores:
        store.wait()
    for q in range(quarters):
        for copy in (across_hops[q], sibling_hops[q], relays[q]):
            copy.wait_send()


def finish_kernel(factor_ref, basis_ref, out_ref, bd):
    nb = out_ref.shape[1]
    size = FCAP * nb

    @pl.when(pl.program_id(0) == 0)
    def _():
        bd[...] = jnp.zeros(bd.shape, F32)
        for s in range(FCAP):
            bd[s * nb : (s + 1) * nb, s * nb : (s + 1) * nb] = unpack(factor_ref[s])

    d1, d2 = split2(bd[...])
    p1 = mm(jnp.concatenate([d1, d2], axis=0), basis_ref[0, 0])
    modes = p1[:size] + (p1[size:] + mm(d1, basis_ref[0, 1]))
    for s in range(FCAP):
        for c in range(2):
            out_ref[s, :, c, :] = modes[s * nb : (s + 1) * nb, c * QP : (c + 1) * QP]


def local(tms, sps, snapshots, block_starts, owner):
    samples, points = snapshots.shape
    blocks = block_starts.shape[0]
    nb = blocks * tms
    size = FCAP * nb
    quarters = points // QP
    table = jnp.asarray(dft_table())
    vm = pltpu.VMEM
    dma = pltpu.SemaphoreType.DMA
    basis, factors = pl.pallas_call(
        functools.partial(kernel, tms, sps),
        out_shape=[
            jax.ShapeDtypeStruct((quarters, 2, size, 2 * QP), BF16),
            jax.ShapeDtypeStruct((FCAP, nb // 4, nb * 4), F32),
        ],
        in_specs=[pl.BlockSpec(memory_space=pltpu.HBM)] * 4,
        out_specs=[
            pl.BlockSpec(memory_space=pltpu.HBM),
            pl.BlockSpec(memory_space=pltpu.VMEM),
        ],
        scratch_shapes=[
            pltpu.SMEM((blocks,), jnp.int32),
            pltpu.SMEM((NF,), jnp.int32),
            vm((ROWS, NFFT), F32),
            vm((quarters, samples, QP), F32),
            vm((ROWS, blocks, samples), F32),
            vm((3 * ROWS * blocks, samples), BF16),
            vm((NF + 1, blocks, 2 * QP), F32),
            vm((quarters, 2, FCAP, blocks, 2 * QP), F32),
            vm((quarters, PAIR_CAP, blocks, 2 * QP), F32),
            vm((quarters, FCAP, blocks, 2 * QP), F32),
            vm((tms, FCAP, blocks, 2 * QP), F32),
            vm((quarters, 3, size, 2 * QP), BF16),
            vm((quarters, 2, size, 2 * QP), BF16),
            vm((size, size), F32),
            vm((2, FCAP, nb // 4, nb * 4), F32),
            vm((2, sps, nb // 4, nb * 4), F32),
            vm((2, nb // 4, nb * 4), F32),
            vm((2, FCAP, nb // 4, nb * 4), F32),
            vm((size, size), F32),
            dma((3,)),
            dma((quarters,)),
            dma((quarters, 3)),
            dma((quarters, 3)),
            dma((2, FCAP)),
            dma((2, sps)),
            dma((2, sps)),
            dma((2, FCAP)),
            *[vm((2, PAIR_CAP, blocks, 2 * QP), F32) for _ in range(quarters)],
        ],
        compiler_params=pltpu.CompilerParams(
            collective_id=0, has_side_effects=True, vmem_limit_bytes=VMEM_BYTES
        ),
    )(block_starts, owner, table, snapshots)
    return pl.pallas_call(
        finish_kernel,
        grid=(quarters,),
        out_shape=jax.ShapeDtypeStruct((FCAP, nb, 2, points), F32),
        in_specs=[
            pl.BlockSpec((FCAP, nb // 4, nb * 4), lambda q: (0, 0, 0)),
            pl.BlockSpec((1, 2, size, 2 * QP), lambda q: (q, 0, 0, 0)),
        ],
        out_specs=pl.BlockSpec((FCAP, nb, 2, QP), lambda q: (0, 0, 0, q)),
        scratch_shapes=[vm((size, size), F32)],
        compiler_params=pltpu.CompilerParams(vmem_limit_bytes=VMEM_BYTES),
    )(factors, basis)


def solution(mesh):
    placed = (P("tm", "space"), P("tm"), P())
    return jax.shard_map(
        functools.partial(local, mesh.shape["tm"], mesh.shape["space"]),
        mesh=mesh, in_specs=placed, out_specs=P("tm", None, None, "space"), check_vma=False,
    )
```

```python
import functools

import jax
import jax.numpy as jnp
import numpy as np
from jax import lax
from jax.experimental import pallas as pl
from jax.experimental.pallas import tpu as pltpu
from jax.sharding import PartitionSpec as P

NFFT = 256
NF = 9
FCAP = 5
PAIR_CAP = 7
GAP = 112
VMEM_BYTES = 64 * 1024 * 1024 - 65536
ROWS = 2 * NF
QP = 256
F32 = jnp.float32
BF16 = jnp.bfloat16
MESH = pl.DeviceIdType.MESH


def dft_table():
    times = np.arange(NFFT)
    phase = (np.arange(NF)[:, None] * times[None, :]) % NFFT
    angle = 2.0 * np.pi / NFFT * phase
    window = 0.5 - 0.5 * np.cos(2.0 * np.pi / NFFT * times)
    table = np.stack([window * np.cos(angle), -window * np.sin(angle)], axis=1)
    return table.reshape(ROWS, NFFT).astype(np.float32)


def split3(x):
    a = x.astype(BF16)
    rest = x - a.astype(F32)
    b = rest.astype(BF16)
    c = (rest - b.astype(F32)).astype(BF16)
    return a, b, c


def split2(x):
    a = x.astype(BF16)
    return a, (x - a.astype(F32)).astype(BF16)


def mm(a, b):
    return jnp.dot(a, b, preferred_element_type=F32)


def mm_t(a, b):
    return lax.dot_general(a, b, (((1,), (1,)), ((), ())), preferred_element_type=F32)


def pack(square):
    n = square.shape[0] // 4
    return jnp.concatenate([square[n * i : n * i + n] for i in range(4)], axis=1)


def unpack(packed):
    n = packed.shape[1] // 4
    return jnp.concatenate([packed[:, n * i : n * i + n] for i in range(4)], axis=0)


def inverse_factor(gram, empty, panel=8):
    n = gram.shape[0]
    row = lax.broadcasted_iota(jnp.int32, (n, n), 0)
    col = lax.broadcasted_iota(jnp.int32, (n, n), 1)
    eye = jnp.where(row == col, 1.0, 0.0).astype(F32)
    gram = gram + jnp.where(empty, 1.0, 0.0) * eye
    work = jnp.concatenate([eye, gram, jnp.zeros((n, 128 - 2 * n), F32)], axis=1)
    rows = lax.broadcasted_iota(jnp.int32, (n, 128), 0)
    diag = jnp.ones((n, 128), F32)
    for first in range(0, n, panel):
        cols = [
            jnp.broadcast_to(work[:, n + first + j : n + first + j + 1], (n, 128))
            for j in range(panel)
        ]
        for j in range(panel):
            k = first + j
            pivot = jnp.broadcast_to(cols[j][k : k + 1], (n, 128))
            diag = jnp.where(rows == k, pivot, diag)
            factor = jnp.where(rows > k, cols[j] * (1.0 / cols[j][k : k + 1]), 0.0)
            work = work - factor * work[k : k + 1]
            for i in range(j + 1, panel):
                cols[i] = cols[i] - factor * cols[i][k : k + 1]
    return (work / jnp.sqrt(diag))[:, :n]


def kernel(
    tms, sps, starts_hbm, owner_hbm, tab_hbm, snap_hbm, basis_out, factor_out,
    starts_ref, owner_ref, tab_ref, snap, tallf, tall, spec, near, far, sib_in, xbuf,
    xs, bs, gacc, packed, gbuf, pinv, ibuf, bd,
    in_sem, snap_sem, a2a_send, a2a_recv, g_send, g_recv, i_send, i_recv, *far_in,
):
    quarters, samples = snap.shape[0], snap.shape[1]
    blocks = starts_hbm.shape[0]
    nb = blocks * tms
    rows_total = 2.0 * quarters * QP * sps
    me = lax.axis_index("tm")
    my = lax.axis_index("space")
    first_worker = sps // 4
    pair, half = me // 2, me % 2
    sibling = 2 * pair + (1 - half)
    across = 2 * (1 - pair) + half
    across_sibling = 2 * (1 - pair) + (1 - half)

    small = [
        pltpu.make_async_copy(source, target, in_sem.at[i])
        for i, (source, target) in enumerate(
            [(starts_hbm, starts_ref), (owner_hbm, owner_ref), (tab_hbm, tab_ref)]
        )
    ]
    for load in small:
        load.start()
    loads = [
        pltpu.make_async_copy(snap_hbm.at[:, pl.ds(q * QP, QP)], snap.at[q], snap_sem.at[q])
        for q in range(quarters)
    ]
    for load in loads:
        load.start()
    barrier = pltpu.get_barrier_semaphore()
    for peer in (sibling, across):
        pl.semaphore_signal(barrier, inc=1, device_id={"tm": peer}, device_id_type=MESH)
    for r in range(1, sps):
        pl.semaphore_signal(barrier, inc=1, device_id={"space": lax.rem(my + r, sps)}, device_id_type=MESH)
    tallf[...] = jnp.zeros(tallf.shape, F32)
    for load in small:
        load.wait()

    span = 2 * NFFT
    wide = jnp.concatenate([tab_ref[...], jnp.zeros((ROWS, span - NFFT), F32)], axis=1)
    for k in range(blocks):
        base = k * GAP // 128 * 128
        keep = min(span, samples - base)
        moved = pltpu.roll(wide, starts_ref[k] - me * samples - base, 1)
        tallf[:, k, base : base + keep] = moved[:, :keep]
    tall[...] = jnp.concatenate(split3(tallf[...].reshape(ROWS * blocks, samples)), axis=0)

    owners = [owner_ref[f] for f in range(NF)]
    owner_pair = [jnp.where(owners[f] >= 2, 1, 0) for f in range(NF)]
    rank, pair_rank = [], []
    for f in range(NF):
        rank.append(sum([jnp.where(owners[g] == owners[f], 1, 0) for g in range(f)], jnp.int32(0)))
        pair_rank.append(
            sum([jnp.where(owner_pair[g] == owner_pair[f], 1, 0) for g in range(f)], jnp.int32(0))
        )

    def owned(holder, s):
        freq, place = jnp.int32(NF), jnp.int32(0)
        for f in range(NF):
            hit = (owners[f] == holder) & (rank[f] == s)
            freq = jnp.where(hit, f, freq)
            place = jnp.where(hit, pair_rank[f], place)
        return freq, place

    held = [owned(me, s) for s in range(FCAP)]
    theirs = [owned(sibling, s)[0] for s in range(FCAP)]
    distant = []
    for place in range(PAIR_CAP):
        freq = jnp.int32(NF)
        for f in range(NF):
            freq = jnp.where((owner_pair[f] == 1 - pair) & (pair_rank[f] == place), f, freq)
        distant.append(freq)
    spec[NF] = jnp.zeros(spec.shape[1:], F32)
    gacc[...] = jnp.zeros(gacc.shape, F32)
    bd[...] = jnp.zeros(bd.shape, F32)

    def hop(source, target, kind, q, peer):
        return pltpu.make_async_remote_copy(
            src_ref=source, dst_ref=target,
            send_sem=a2a_send.at[q, kind], recv_sem=a2a_recv.at[q, kind],
            device_id={"tm": peer}, device_id_type=MESH,
        )

    across_hops = [hop(far.at[q], far_in[q].at[0], 0, q, across) for q in range(quarters)]
    sibling_hops = [hop(near.at[q, 1], sib_in.at[q], 1, q, sibling) for q in range(quarters)]
    relays = [hop(far_in[q].at[0], far_in[q].at[1], 2, q, sibling) for q in range(quarters)]
    m = ROWS * blocks
    for q in range(quarters):
        loads[q].wait()
        s1, s2, s3 = split3(snap[q])
        p1 = mm(tall[...], s1)
        p2 = mm(tall[: 2 * m], s2)
        p3 = mm(tall[:m], s3)
        spectrum = p1[:m] + ((p1[m : 2 * m] + p2[:m]) + ((p1[2 * m :] + p2[m:]) + p3))
        for f in range(NF):
            for c in range(2):
                at = (2 * f + c) * blocks
                spec[f, :, c * QP : (c + 1) * QP] = spectrum[at : at + blocks]
        for place in range(PAIR_CAP):
            far[q, place] = spec[distant[place]]
        if q == 0:
            pl.semaphore_wait(barrier, sps + 1)
        across_hops[q].start()
        for s in range(FCAP):
            near[q, 0, s] = spec[held[s][0]]
            near[q, 1, s] = spec[theirs[s]]
        sibling_hops[q].start()

    def reduce_and_factor(turn):
        for s in range(FCAP):
            sl = pl.ds(s * nb, nb)
            packed[turn, s] = pack(gacc[sl, sl])
        for s in range(FCAP):
            worker = first_worker + s

            @pl.when(my != worker)
            def _():
                pltpu.make_async_remote_copy(
                    src_ref=packed.at[turn, s], dst_ref=gbuf.at[turn, my],
                    send_sem=g_send.at[turn, s], recv_sem=g_recv.at[turn, my],
                    device_id={"space": worker}, device_id_type=MESH,
                ).start()

        @pl.when((my >= first_worker) & (my < first_worker + FCAP))
        def _():
            mine = my - first_worker
            gbuf[turn, my] = packed[turn, mine]
            for r in range(1, sps):
                source = lax.rem(my + r, sps)
                pltpu.make_async_remote_copy(
                    src_ref=packed.at[turn, 0], dst_ref=gbuf.at[turn, source],
                    send_sem=g_send.at[turn, 0], recv_sem=g_recv.at[turn, source],
                    device_id={"space": source}, device_id_type=MESH,
                ).wait_recv()
            total = gbuf[turn, 0]
            for source in range(1, sps):
                total = total + gbuf[turn, source]
            freq = held[0][0]
            for s in range(1, FCAP):
                freq = jnp.where(mine == s, held[s][0], freq)
            empty = freq == NF
            inverse = pack(inverse_factor(unpack(total * (1.0 / rows_total)), empty))
            pinv[turn] = inverse
            ibuf[turn, mine] = inverse
            copies = []
            for r in range(1, sps):
                peer = lax.rem(my + r, sps)
                copies.append(
                    pltpu.make_async_remote_copy(
                        src_ref=pinv.at[turn], dst_ref=ibuf.at[turn, mine],
                        send_sem=i_send.at[turn, r], recv_sem=i_recv.at[turn, mine],
                        device_id={"space": peer}, device_id_type=MESH,
                    )
                )
                copies[-1].start()
            for copy in copies:
                copy.wait_send()

        for s in range(FCAP):
            worker = first_worker + s

            @pl.when(my != worker)
            def _():
                pltpu.make_async_remote_copy(
                    src_ref=packed.at[turn, s], dst_ref=ibuf.at[turn, s],
                    send_sem=g_send.at[turn, s], recv_sem=i_recv.at[turn, s],
                    device_id={"space": worker}, device_id_type=MESH,
                ).wait()

            if turn == 0:
                bd[s * nb : (s + 1) * nb, s * nb : (s + 1) * nb] = unpack(ibuf[turn, s])
            else:
                factor_out[s] = ibuf[turn, s]

    size = FCAP * nb
    across_hops[0].wait_recv()
    relays[0].start()
    for q in range(quarters):
        if q + 1 < quarters:
            across_hops[q + 1].wait_recv()
            relays[q + 1].start()
        sibling_hops[q].wait_recv()
        relays[q].wait_recv()
        xbuf[me] = near[q, 0]
        xbuf[sibling] = sib_in[q]
        for s in range(FCAP):
            freq, place = held[s]
            xbuf[across, s] = jnp.where(freq < NF, far_in[q][0, place], 0.0)
            xbuf[across_sibling, s] = jnp.where(freq < NF, far_in[q][1, place], 0.0)
        stacked = jnp.concatenate(
            [xbuf[:, s].reshape(nb, 2 * QP) for s in range(FCAP)], axis=0
        )
        x1, x2, x3 = split3(stacked)
        xs[q, 0], xs[q, 1], xs[q, 2] = x1, x2, x3
        p1 = mm_t(xs[q].reshape(3 * size, 2 * QP), x1)
        p2 = mm_t(xs[q, :2].reshape(2 * size, 2 * QP), x2)
        p3 = mm_t(x1, x3)
        gacc[...] += p1[:size] + (
            (p1[size : 2 * size] + p2[:size]) + ((p1[2 * size :] + p2[size:]) + p3)
        )
    reduce_and_factor(0)

    d1, d2, d3 = split3(bd[...])
    d321 = jnp.concatenate([d1, d2, d3], axis=0)
    gacc[...] = jnp.zeros(gacc.shape, F32)
    stores = [
        pltpu.make_async_copy(bs.at[q], basis_out.at[q], snap_sem.at[q]) for q in range(quarters)
    ]
    for q in range(quarters):
        p1 = mm(d321, xs[q, 0])
        p2 = mm(d321[: 2 * size], xs[q, 1])
        p3 = mm(d1, xs[q, 2])
        basis = p1[:size] + (
            (p1[size : 2 * size] + p2[:size]) + ((p1[2 * size :] + p2[size:]) + p3)
        )
        b1, b2 = split2(basis)
        bs[q, 0], bs[q, 1] = b1, b2
        stores[q].start()
        p1 = mm_t(bs[q].reshape(2 * size, 2 * QP), b1)
        gacc[...] += p1[:size] + (p1[size:] + mm_t(b1, b2))
    reduce_and_factor(1)

    for store in stores:
        store.wait()
    for q in range(quarters):
        for copy in (across_hops[q], sibling_hops[q], relays[q]):
            copy.wait_send()


def finish_kernel(factor_ref, basis_ref, out_ref):
    quarters = basis_ref.shape[0]
    nb = basis_ref.shape[2]
    tiles = quarters * QP // 128
    d1, d2 = split2(unpack(factor_ref[0]))
    d21 = jnp.concatenate([d1, d2], axis=0)
    for q in range(quarters):
        p1 = mm(d21, basis_ref[q, 0])
        modes = p1[:nb] + (p1[nb:] + mm(d1, basis_ref[q, 1]))
        for c in range(2):
            for t in range(QP // 128):
                at = 2 * (q * (QP // 128) + t) + c
                lane = c * QP + t * 128
                out_ref[pl.ds(at, nb, stride=2 * tiles), :] = modes[:, lane : lane + 128]


def local(tms, sps, snapshots, block_starts, owner):
    samples, points = snapshots.shape
    blocks = block_starts.shape[0]
    nb = blocks * tms
    size = FCAP * nb
    quarters = points // QP
    table = jnp.asarray(dft_table())
    vm = pltpu.VMEM
    dma = pltpu.SemaphoreType.DMA
    basis, factors = pl.pallas_call(
        functools.partial(kernel, tms, sps),
        out_shape=[
            jax.ShapeDtypeStruct((quarters, 2, size, 2 * QP), BF16),
            jax.ShapeDtypeStruct((FCAP, nb // 4, nb * 4), F32),
        ],
        in_specs=[pl.BlockSpec(memory_space=pltpu.HBM)] * 4,
        out_specs=[
            pl.BlockSpec(memory_space=pltpu.HBM),
            pl.BlockSpec(memory_space=pltpu.VMEM),
        ],
        scratch_shapes=[
            pltpu.SMEM((blocks,), jnp.int32),
            pltpu.SMEM((NF,), jnp.int32),
            vm((ROWS, NFFT), F32),
            vm((quarters, samples, QP), F32),
            vm((ROWS, blocks, samples), F32),
            vm((3 * ROWS * blocks, samples), BF16),
            vm((NF + 1, blocks, 2 * QP), F32),
            vm((quarters, 2, FCAP, blocks, 2 * QP), F32),
            vm((quarters, PAIR_CAP, blocks, 2 * QP), F32),
            vm((quarters, FCAP, blocks, 2 * QP), F32),
            vm((tms, FCAP, blocks, 2 * QP), F32),
            vm((quarters, 3, size, 2 * QP), BF16),
            vm((quarters, 2, size, 2 * QP), BF16),
            vm((size, size), F32),
            vm((2, FCAP, nb // 4, nb * 4), F32),
            vm((2, sps, nb // 4, nb * 4), F32),
            vm((2, nb // 4, nb * 4), F32),
            vm((2, FCAP, nb // 4, nb * 4), F32),
            vm((size, size), F32),
            dma((3,)),
            dma((quarters,)),
            dma((quarters, 3)),
            dma((quarters, 3)),
            dma((2, FCAP)),
            dma((2, sps)),
            dma((2, sps)),
            dma((2, FCAP)),
            *[vm((2, PAIR_CAP, blocks, 2 * QP), F32) for _ in range(quarters)],
        ],
        compiler_params=pltpu.CompilerParams(
            collective_id=0, has_side_effects=True, vmem_limit_bytes=VMEM_BYTES
        ),
    )(block_starts, owner, table, snapshots)
    tiles = points // 128
    modes = pl.pallas_call(
        finish_kernel,
        grid=(FCAP,),
        out_shape=jax.ShapeDtypeStruct((size * tiles * 2, 128), F32),
        in_specs=[
            pl.BlockSpec((1, nb // 4, nb * 4), lambda s: (s, 0, 0)),
            pl.BlockSpec((quarters, 2, nb, 2 * QP), lambda s: (0, 0, s, 0)),
        ],
        out_specs=pl.BlockSpec((nb * tiles * 2, 128), lambda s: (s, 0)),
        compiler_params=pltpu.CompilerParams(vmem_limit_bytes=VMEM_BYTES),
    )(factors, basis)
    modes = modes.reshape(FCAP, nb, tiles, 2, 128).transpose(0, 1, 3, 2, 4)
    return modes.reshape(FCAP, nb, 2, points)


def solution(mesh):
    placed = (P("tm", "space"), P("tm"), P())
    return jax.shard_map(
        functools.partial(local, mesh.shape["tm"], mesh.shape["space"]),
        mesh=mesh, in_specs=placed, out_specs=P("tm", None, None, "space"), check_vma=False,
    )
```

```python
import functools

import jax
import jax.numpy as jnp
import numpy as np
from jax import lax
from jax.experimental import pallas as pl
from jax.experimental.pallas import tpu as pltpu
from jax.sharding import PartitionSpec as P

NFFT = 256
NF = 9
FCAP = 5
PAIR_CAP = 7
GAP = 112
VMEM_BYTES = 64 * 1024 * 1024 - 65536
ROWS = 2 * NF
QP = 256
F32 = jnp.float32
BF16 = jnp.bfloat16
MESH = pl.DeviceIdType.MESH


def dft_table():
    times = np.arange(NFFT)
    phase = (np.arange(NF)[:, None] * times[None, :]) % NFFT
    angle = 2.0 * np.pi / NFFT * phase
    window = 0.5 - 0.5 * np.cos(2.0 * np.pi / NFFT * times)
    table = np.stack([window * np.cos(angle), -window * np.sin(angle)], axis=1)
    return table.reshape(ROWS, NFFT).astype(np.float32)


def split3(x):
    a = x.astype(BF16)
    rest = x - a.astype(F32)
    b = rest.astype(BF16)
    c = (rest - b.astype(F32)).astype(BF16)
    return a, b, c


def split2(x):
    a = x.astype(BF16)
    return a, (x - a.astype(F32)).astype(BF16)


def mm(a, b):
    return jnp.dot(a, b, preferred_element_type=F32)


def mm_t(a, b):
    return lax.dot_general(a, b, (((1,), (1,)), ((), ())), preferred_element_type=F32)


def pack(square):
    n = square.shape[0] // 4
    return jnp.concatenate([square[n * i : n * i + n] for i in range(4)], axis=1)


def unpack(packed):
    n = packed.shape[1] // 4
    return jnp.concatenate([packed[:, n * i : n * i + n] for i in range(4)], axis=0)


def inverse_factor(gram, empty, panel=8):
    n = gram.shape[0]
    row = lax.broadcasted_iota(jnp.int32, (n, n), 0)
    col = lax.broadcasted_iota(jnp.int32, (n, n), 1)
    eye = jnp.where(row == col, 1.0, 0.0).astype(F32)
    gram = gram + jnp.where(empty, 1.0, 0.0) * eye
    work = jnp.concatenate([eye, gram, jnp.zeros((n, 128 - 2 * n), F32)], axis=1)
    rows = lax.broadcasted_iota(jnp.int32, (n, 128), 0)
    diag = jnp.ones((n, 128), F32)
    for first in range(0, n, panel):
        cols = [
            jnp.broadcast_to(work[:, n + first + j : n + first + j + 1], (n, 128))
            for j in range(panel)
        ]
        for j in range(panel):
            k = first + j
            pivot = jnp.broadcast_to(cols[j][k : k + 1], (n, 128))
            diag = jnp.where(rows == k, pivot, diag)
            factor = jnp.where(rows > k, cols[j] * (1.0 / cols[j][k : k + 1]), 0.0)
            work = work - factor * work[k : k + 1]
            for i in range(j + 1, panel):
                cols[i] = cols[i] - factor * cols[i][k : k + 1]
    return (work / jnp.sqrt(diag))[:, :n]


def kernel(
    tms, sps, starts_hbm, owner_hbm, tab_hbm, snap_hbm, out_ref,
    starts_ref, owner_ref, tab_ref, snap, tallf, tall, spec, near, far, sib_in, xbuf,
    xs, bs, gacc, packed, gbuf, pinv, ibuf, bd, parts,
    in_sem, snap_sem, a2a_send, a2a_recv, g_send, g_recv, i_send, i_recv, far_in, stage,
):
    quarters, samples = snap.shape[0], snap.shape[1]
    blocks = starts_hbm.shape[0]
    nb = blocks * tms
    rows_total = 2.0 * quarters * QP * sps
    me = lax.axis_index("tm")
    my = lax.axis_index("space")
    first_worker = sps // 4
    pair, half = me // 2, me % 2
    sibling = 2 * pair + (1 - half)
    across = 2 * (1 - pair) + half
    across_sibling = 2 * (1 - pair) + (1 - half)

    small = [
        pltpu.make_async_copy(source, target, in_sem.at[i])
        for i, (source, target) in enumerate(
            [(starts_hbm, starts_ref), (owner_hbm, owner_ref), (tab_hbm, tab_ref)]
        )
    ]
    for load in small:
        load.start()
    def snap_load(q):
        lanes = pl.ds(pl.multiple_of(q * QP, QP), QP)
        return pltpu.make_async_copy(snap_hbm.at[:, lanes], snap.at[q], snap_sem.at[q])

    for q in range(quarters):
        snap_load(q).start()
    barrier = pltpu.get_barrier_semaphore()
    for peer in (sibling, across):
        pl.semaphore_signal(barrier, inc=1, device_id={"tm": peer}, device_id_type=MESH)
    for r in range(1, sps):
        pl.semaphore_signal(barrier, inc=1, device_id={"space": lax.rem(my + r, sps)}, device_id_type=MESH)
    tallf[...] = jnp.zeros(tallf.shape, F32)
    for load in small:
        load.wait()

    span = 2 * NFFT
    wide = jnp.concatenate([tab_ref[...], jnp.zeros((ROWS, span - NFFT), F32)], axis=1)
    for k in range(blocks):
        base = k * GAP // 128 * 128
        keep = min(span, samples - base)
        moved = pltpu.roll(wide, starts_ref[k] - me * samples - base, 1)
        tallf[:, k, base : base + keep] = moved[:, :keep]
    tall[...] = jnp.concatenate(split3(tallf[...].reshape(ROWS * blocks, samples)), axis=0)

    owners = [owner_ref[f] for f in range(NF)]
    owner_pair = [jnp.where(owners[f] >= 2, 1, 0) for f in range(NF)]
    rank, pair_rank = [], []
    for f in range(NF):
        rank.append(sum([jnp.where(owners[g] == owners[f], 1, 0) for g in range(f)], jnp.int32(0)))
        pair_rank.append(
            sum([jnp.where(owner_pair[g] == owner_pair[f], 1, 0) for g in range(f)], jnp.int32(0))
        )

    def owned(holder, s):
        freq, place = jnp.int32(NF), jnp.int32(0)
        for f in range(NF):
            hit = (owners[f] == holder) & (rank[f] == s)
            freq = jnp.where(hit, f, freq)
            place = jnp.where(hit, pair_rank[f], place)
        return freq, place

    held = [owned(me, s) for s in range(FCAP)]
    theirs = [owned(sibling, s)[0] for s in range(FCAP)]
    distant = []
    for place in range(PAIR_CAP):
        freq = jnp.int32(NF)
        for f in range(NF):
            freq = jnp.where((owner_pair[f] == 1 - pair) & (pair_rank[f] == place), f, freq)
        distant.append(freq)
    spec[NF] = jnp.zeros(spec.shape[1:], F32)
    gacc[...] = jnp.zeros(gacc.shape, F32)
    bd[...] = jnp.zeros(bd.shape, F32)

    def hop(source, target, kind, q, peer):
        return pltpu.make_async_remote_copy(
            src_ref=source, dst_ref=target,
            send_sem=a2a_send.at[q, kind], recv_sem=a2a_recv.at[q, kind],
            device_id={"tm": peer}, device_id_type=MESH,
        )

    def across_hop(q):
        return hop(far.at[q], far_in.at[q, 0], 0, q, across)

    def sibling_hop(q):
        return hop(near.at[q, 1], sib_in.at[q], 1, q, sibling)

    def relay(q):
        return hop(far_in.at[q, 0], far_in.at[q, 1], 2, q, sibling)

    m = ROWS * blocks
    pl.semaphore_wait(barrier, sps + 1)

    @pl.loop(0, quarters)
    def _(q):
        snap_load(q).wait()
        s1, s2, s3 = split3(snap[q])
        p1 = mm(tall[...], s1)
        p2 = mm(tall[: 2 * m], s2)
        p3 = mm(tall[:m], s3)
        spectrum = p1[:m] + ((p1[m : 2 * m] + p2[:m]) + ((p1[2 * m :] + p2[m:]) + p3))
        for f in range(NF):
            for c in range(2):
                at = (2 * f + c) * blocks
                spec[f, :, c * QP : (c + 1) * QP] = spectrum[at : at + blocks]
        for place in range(PAIR_CAP):
            far[q, place] = spec[distant[place]]
        across_hop(q).start()
        for s in range(FCAP):
            near[q, 0, s] = spec[held[s][0]]
            near[q, 1, s] = spec[theirs[s]]
        sibling_hop(q).start()

    def reduce_and_factor(turn):
        for s in range(FCAP):
            sl = pl.ds(s * nb, nb)
            packed[turn, s] = pack(gacc[sl, sl])
        for s in range(FCAP):
            worker = first_worker + s

            @pl.when(my != worker)
            def _():
                pltpu.make_async_remote_copy(
                    src_ref=packed.at[turn, s], dst_ref=gbuf.at[turn, my],
                    send_sem=g_send.at[turn, s], recv_sem=g_recv.at[turn, my],
                    device_id={"space": worker}, device_id_type=MESH,
                ).start()

        @pl.when((my >= first_worker) & (my < first_worker + FCAP))
        def _():
            mine = my - first_worker
            gbuf[turn, my] = packed[turn, mine]
            for r in range(1, sps):
                source = lax.rem(my + r, sps)
                pltpu.make_async_remote_copy(
                    src_ref=packed.at[turn, 0], dst_ref=gbuf.at[turn, source],
                    send_sem=g_send.at[turn, 0], recv_sem=g_recv.at[turn, source],
                    device_id={"space": source}, device_id_type=MESH,
                ).wait_recv()
            total = gbuf[turn, 0]
            for source in range(1, sps):
                total = total + gbuf[turn, source]
            freq = held[0][0]
            for s in range(1, FCAP):
                freq = jnp.where(mine == s, held[s][0], freq)
            empty = freq == NF
            inverse = pack(inverse_factor(unpack(total * (1.0 / rows_total)), empty))
            pinv[turn] = inverse
            ibuf[turn, mine] = inverse
            copies = []
            for r in range(1, sps):
                peer = lax.rem(my + r, sps)
                copies.append(
                    pltpu.make_async_remote_copy(
                        src_ref=pinv.at[turn], dst_ref=ibuf.at[turn, mine],
                        send_sem=i_send.at[turn, r], recv_sem=i_recv.at[turn, mine],
                        device_id={"space": peer}, device_id_type=MESH,
                    )
                )
                copies[-1].start()
            for copy in copies:
                copy.wait_send()

        for s in range(FCAP):
            worker = first_worker + s

            @pl.when(my != worker)
            def _():
                pltpu.make_async_remote_copy(
                    src_ref=packed.at[turn, s], dst_ref=ibuf.at[turn, s],
                    send_sem=g_send.at[turn, s], recv_sem=i_recv.at[turn, s],
                    device_id={"space": worker}, device_id_type=MESH,
                ).wait()

            bd[s * nb : (s + 1) * nb, s * nb : (s + 1) * nb] = unpack(ibuf[turn, s])

    size = FCAP * nb
    across_hop(0).wait_recv()
    relay(0).start()

    @pl.loop(0, quarters)
    def _(q):
        @pl.when(q + 1 < quarters)
        def _():
            across_hop(q + 1).wait_recv()
            relay(q + 1).start()

        sibling_hop(q).wait_recv()
        xbuf[me] = near[q, 0]
        xbuf[sibling] = sib_in[q]
        relay(q).wait_recv()
        stage[...] = far_in[q]
        for s in range(FCAP):
            freq, place = held[s]
            xbuf[across, s] = jnp.where(freq < NF, stage[0, place], 0.0)
            xbuf[across_sibling, s] = jnp.where(freq < NF, stage[1, place], 0.0)
        stacked = jnp.concatenate(
            [xbuf[:, s].reshape(nb, 2 * QP) for s in range(FCAP)], axis=0
        )
        x1, x2, x3 = split3(stacked)
        xs[q, 0], xs[q, 1], xs[q, 2] = x1, x2, x3
        p1 = mm_t(xs[q].reshape(3 * size, 2 * QP), x1)
        p2 = mm_t(xs[q, :2].reshape(2 * size, 2 * QP), x2)
        p3 = mm_t(x1, x3)
        gacc[...] += p1[:size] + (
            (p1[size : 2 * size] + p2[:size]) + ((p1[2 * size :] + p2[size:]) + p3)
        )

    reduce_and_factor(0)

    d1, d2, d3 = split3(bd[...])
    parts[...] = jnp.concatenate([d1, d2, d3], axis=0)
    gacc[...] = jnp.zeros(gacc.shape, F32)

    @pl.loop(0, quarters)
    def _(q):
        p1 = mm(parts[...], xs[q, 0])
        p2 = mm(parts[: 2 * size], xs[q, 1])
        p3 = mm(parts[:size], xs[q, 2])
        basis = p1[:size] + (
            (p1[size : 2 * size] + p2[:size]) + ((p1[2 * size :] + p2[size:]) + p3)
        )
        b1, b2 = split2(basis)
        bs[q, 0], bs[q, 1] = b1, b2
        p1 = mm_t(bs[q].reshape(2 * size, 2 * QP), b1)
        gacc[...] += p1[:size] + (p1[size:] + mm_t(b1, b2))

    reduce_and_factor(1)

    d1, d2 = split2(bd[...])
    parts[: 2 * size] = jnp.concatenate([d1, d2], axis=0)
    tiles = quarters * QP // 128

    @pl.loop(0, quarters)
    def _(q):
        p1 = mm(parts[: 2 * size], bs[q, 0])
        modes = p1[:size] + (p1[size:] + mm(parts[:size], bs[q, 1]))
        for c in range(2):
            for t in range(QP // 128):
                at = 2 * (q * (QP // 128) + t) + c
                lane = c * QP + t * 128
                out_ref[pl.ds(at, size, stride=2 * tiles), :] = modes[:, lane : lane + 128]

    @pl.loop(0, quarters)
    def _(q):
        across_hop(q).wait_send()
        sibling_hop(q).wait_send()
        relay(q).wait_send()


def hand_over(source, target, sem):
    chunks = sem.shape[0]
    rows = source.shape[0] // chunks
    copies = [
        pltpu.make_async_copy(
            source.at[pl.ds(i * rows, rows)], target.at[pl.ds(i * rows, rows)], sem.at[i]
        )
        for i in range(chunks)
    ]
    for copy in copies:
        copy.start()
    for copy in copies:
        copy.wait()


def local(tms, sps, snapshots, block_starts, owner):
    samples, points = snapshots.shape
    blocks = block_starts.shape[0]
    nb = blocks * tms
    size = FCAP * nb
    quarters = points // QP
    tiles = points // 128
    table = jnp.asarray(dft_table())
    vm = pltpu.VMEM
    dma = pltpu.SemaphoreType.DMA
    modes = pl.pallas_call(
        functools.partial(kernel, tms, sps),
        out_shape=jax.ShapeDtypeStruct((size * tiles * 2, 128), F32),
        in_specs=[pl.BlockSpec(memory_space=pltpu.HBM)] * 4,
        out_specs=pl.BlockSpec(memory_space=pltpu.VMEM),
        scratch_shapes=[
            pltpu.SMEM((blocks,), jnp.int32),
            pltpu.SMEM((NF,), jnp.int32),
            vm((ROWS, NFFT), F32),
            vm((quarters, samples, QP), F32),
            vm((ROWS, blocks, samples), F32),
            vm((3 * ROWS * blocks, samples), BF16),
            vm((NF + 1, blocks, 2 * QP), F32),
            vm((quarters, 2, FCAP, blocks, 2 * QP), F32),
            vm((quarters, PAIR_CAP, blocks, 2 * QP), F32),
            vm((quarters, FCAP, blocks, 2 * QP), F32),
            vm((tms, FCAP, blocks, 2 * QP), F32),
            vm((quarters, 3, size, 2 * QP), BF16),
            vm((quarters, 2, size, 2 * QP), BF16),
            vm((size, size), F32),
            vm((2, FCAP, nb // 4, nb * 4), F32),
            vm((2, sps, nb // 4, nb * 4), F32),
            vm((2, nb // 4, nb * 4), F32),
            vm((2, FCAP, nb // 4, nb * 4), F32),
            vm((size, size), F32),
            vm((3 * size, size), BF16),
            dma((3,)),
            dma((quarters,)),
            dma((quarters, 3)),
            dma((quarters, 3)),
            dma((2, FCAP)),
            dma((2, sps)),
            dma((2, sps)),
            dma((2, FCAP)),
            vm((quarters, 2, PAIR_CAP, blocks, 2 * QP), F32),
            vm((2, PAIR_CAP, blocks, 2 * QP), F32),
        ],
        compiler_params=pltpu.CompilerParams(
            collective_id=0, has_side_effects=True, vmem_limit_bytes=VMEM_BYTES
        ),
    )(block_starts, owner, table, snapshots)
    modes = pl.pallas_call(
        hand_over,
        out_shape=jax.ShapeDtypeStruct(modes.shape, F32),
        in_specs=[pl.BlockSpec(memory_space=pltpu.HBM)],
        out_specs=pl.BlockSpec(memory_space=pltpu.HBM),
        scratch_shapes=[dma((2 * FCAP,))],
        compiler_params=pltpu.CompilerParams(vmem_limit_bytes=VMEM_BYTES),
    )(modes)
    modes = modes.reshape(FCAP, nb, tiles, 2, 128).transpose(0, 1, 3, 2, 4)
    return modes.reshape(FCAP, nb, 2, points)


def solution(mesh):
    placed = (P("tm", "space"), P("tm"), P())
    return jax.shard_map(
        functools.partial(local, mesh.shape["tm"], mesh.shape["space"]),
        mesh=mesh, in_specs=placed, out_specs=P("tm", None, None, "space"), check_vma=False,
    )
```

```python
import functools

import jax
import jax.numpy as jnp
import numpy as np
from jax import lax
from jax.experimental import pallas as pl
from jax.experimental.pallas import tpu as pltpu
from jax.sharding import PartitionSpec as P

NFFT = 256
NF = 9
FCAP = 5
PAIR_CAP = 7
GAP = 112
VMEM_BYTES = 64 * 1024 * 1024 - 65536
ROWS = 2 * NF
QP = 256
F32 = jnp.float32
BF16 = jnp.bfloat16
MESH = pl.DeviceIdType.MESH


def dft_table():
    times = np.arange(NFFT)
    phase = (np.arange(NF)[:, None] * times[None, :]) % NFFT
    angle = 2.0 * np.pi / NFFT * phase
    window = 0.5 - 0.5 * np.cos(2.0 * np.pi / NFFT * times)
    table = np.stack([window * np.cos(angle), -window * np.sin(angle)], axis=1)
    return table.reshape(ROWS, NFFT).astype(np.float32)


def split3(x):
    a = x.astype(BF16)
    rest = x - a.astype(F32)
    b = rest.astype(BF16)
    c = (rest - b.astype(F32)).astype(BF16)
    return a, b, c


def split2(x):
    a = x.astype(BF16)
    return a, (x - a.astype(F32)).astype(BF16)


def mm(a, b):
    return jnp.dot(a, b, preferred_element_type=F32)


def mm_t(a, b):
    return lax.dot_general(a, b, (((1,), (1,)), ((), ())), preferred_element_type=F32)


def pack(square):
    n = square.shape[0] // 4
    return jnp.concatenate([square[n * i : n * i + n] for i in range(4)], axis=1)


def unpack(packed):
    n = packed.shape[1] // 4
    return jnp.concatenate([packed[:, n * i : n * i + n] for i in range(4)], axis=0)


def inverse_factor(gram, empty, panel=8):
    n = gram.shape[0]
    row = lax.broadcasted_iota(jnp.int32, (n, n), 0)
    col = lax.broadcasted_iota(jnp.int32, (n, n), 1)
    eye = jnp.where(row == col, 1.0, 0.0).astype(F32)
    gram = gram + jnp.where(empty, 1.0, 0.0) * eye
    work = jnp.concatenate([eye, gram, jnp.zeros((n, 128 - 2 * n), F32)], axis=1)
    rows = lax.broadcasted_iota(jnp.int32, (n, 128), 0)
    diag = jnp.ones((n, 128), F32)
    for first in range(0, n, panel):
        cols = [
            jnp.broadcast_to(work[:, n + first + j : n + first + j + 1], (n, 128))
            for j in range(panel)
        ]
        for j in range(panel):
            k = first + j
            pivot = jnp.broadcast_to(cols[j][k : k + 1], (n, 128))
            diag = jnp.where(rows == k, pivot, diag)
            factor = jnp.where(rows > k, cols[j] * (1.0 / cols[j][k : k + 1]), 0.0)
            work = work - factor * work[k : k + 1]
            for i in range(j + 1, panel):
                cols[i] = cols[i] - factor * cols[i][k : k + 1]
    return (work / jnp.sqrt(diag))[:, :n]


def kernel(
    tms, sps, starts_hbm, owner_hbm, tab_hbm, snap_hbm, out_ref,
    starts_ref, owner_ref, tab_ref, snap, tallf, tall, spec, near, far, sib_in, xbuf,
    xs, bs, gacc, packed, gbuf, pinv, ibuf, bd,
    in_sem, snap_sem, a2a_send, a2a_recv, g_send, g_recv, i_send, i_recv, *far_in,
):
    quarters, samples = snap.shape[0], snap.shape[1]
    blocks = starts_hbm.shape[0]
    nb = blocks * tms
    rows_total = 2.0 * quarters * QP * sps
    me = lax.axis_index("tm")
    my = lax.axis_index("space")
    first_worker = sps // 4
    pair, half = me // 2, me % 2
    sibling = 2 * pair + (1 - half)
    across = 2 * (1 - pair) + half
    across_sibling = 2 * (1 - pair) + (1 - half)

    small = [
        pltpu.make_async_copy(source, target, in_sem.at[i])
        for i, (source, target) in enumerate(
            [(starts_hbm, starts_ref), (owner_hbm, owner_ref), (tab_hbm, tab_ref)]
        )
    ]
    for load in small:
        load.start()
    loads = [
        pltpu.make_async_copy(snap_hbm.at[:, pl.ds(q * QP, QP)], snap.at[q], snap_sem.at[q])
        for q in range(quarters)
    ]
    for load in loads:
        load.start()
    barrier = pltpu.get_barrier_semaphore()
    for peer in (sibling, across):
        pl.semaphore_signal(barrier, inc=1, device_id={"tm": peer}, device_id_type=MESH)
    for r in range(1, sps):
        pl.semaphore_signal(barrier, inc=1, device_id={"space": lax.rem(my + r, sps)}, device_id_type=MESH)
    tallf[...] = jnp.zeros(tallf.shape, F32)
    for load in small:
        load.wait()

    span = 2 * NFFT
    wide = jnp.concatenate([tab_ref[...], jnp.zeros((ROWS, span - NFFT), F32)], axis=1)
    for k in range(blocks):
        base = k * GAP // 128 * 128
        keep = min(span, samples - base)
        moved = pltpu.roll(wide, starts_ref[k] - me * samples - base, 1)
        tallf[:, k, base : base + keep] = moved[:, :keep]
    tall[...] = jnp.concatenate(split3(tallf[...].reshape(ROWS * blocks, samples)), axis=0)

    owners = [owner_ref[f] for f in range(NF)]
    owner_pair = [jnp.where(owners[f] >= 2, 1, 0) for f in range(NF)]
    rank, pair_rank = [], []
    for f in range(NF):
        rank.append(sum([jnp.where(owners[g] == owners[f], 1, 0) for g in range(f)], jnp.int32(0)))
        pair_rank.append(
            sum([jnp.where(owner_pair[g] == owner_pair[f], 1, 0) for g in range(f)], jnp.int32(0))
        )

    def owned(holder, s):
        freq, place = jnp.int32(NF), jnp.int32(0)
        for f in range(NF):
            hit = (owners[f] == holder) & (rank[f] == s)
            freq = jnp.where(hit, f, freq)
            place = jnp.where(hit, pair_rank[f], place)
        return freq, place

    held = [owned(me, s) for s in range(FCAP)]
    theirs = [owned(sibling, s)[0] for s in range(FCAP)]
    distant = []
    for place in range(PAIR_CAP):
        freq = jnp.int32(NF)
        for f in range(NF):
            freq = jnp.where((owner_pair[f] == 1 - pair) & (pair_rank[f] == place), f, freq)
        distant.append(freq)
    spec[NF] = jnp.zeros(spec.shape[1:], F32)
    gacc[...] = jnp.zeros(gacc.shape, F32)
    bd[...] = jnp.zeros(bd.shape, F32)

    def hop(source, target, kind, q, peer):
        return pltpu.make_async_remote_copy(
            src_ref=source, dst_ref=target,
            send_sem=a2a_send.at[q, kind], recv_sem=a2a_recv.at[q, kind],
            device_id={"tm": peer}, device_id_type=MESH,
        )

    across_hops = [hop(far.at[q], far_in[q].at[0], 0, q, across) for q in range(quarters)]
    sibling_hops = [hop(near.at[q, 1], sib_in.at[q], 1, q, sibling) for q in range(quarters)]
    relays = [hop(far_in[q].at[0], far_in[q].at[1], 2, q, sibling) for q in range(quarters)]
    m = ROWS * blocks
    for q in range(quarters):
        loads[q].wait()
        s1, s2, s3 = split3(snap[q])
        p1 = mm(tall[...], s1)
        p2 = mm(tall[: 2 * m], s2)
        p3 = mm(tall[:m], s3)
        spectrum = p1[:m] + ((p1[m : 2 * m] + p2[:m]) + ((p1[2 * m :] + p2[m:]) + p3))
        for f in range(NF):
            for c in range(2):
                at = (2 * f + c) * blocks
                spec[f, :, c * QP : (c + 1) * QP] = spectrum[at : at + blocks]
        for place in range(PAIR_CAP):
            far[q, place] = spec[distant[place]]
        if q == 0:
            pl.semaphore_wait(barrier, sps + 1)
        across_hops[q].start()
        for s in range(FCAP):
            near[q, 0, s] = spec[held[s][0]]
            near[q, 1, s] = spec[theirs[s]]
        sibling_hops[q].start()

    def reduce_and_factor(turn):
        for s in range(FCAP):
            sl = pl.ds(s * nb, nb)
            packed[turn, s] = pack(gacc[sl, sl])
        for s in range(FCAP):
            worker = first_worker + s

            @pl.when(my != worker)
            def _():
                pltpu.make_async_remote_copy(
                    src_ref=packed.at[turn, s], dst_ref=gbuf.at[turn, my],
                    send_sem=g_send.at[turn, s], recv_sem=g_recv.at[turn, my],
                    device_id={"space": worker}, device_id_type=MESH,
                ).start()

        @pl.when((my >= first_worker) & (my < first_worker + FCAP))
        def _():
            mine = my - first_worker
            gbuf[turn, my] = packed[turn, mine]
            for r in range(1, sps):
                source = lax.rem(my + r, sps)
                pltpu.make_async_remote_copy(
                    src_ref=packed.at[turn, 0], dst_ref=gbuf.at[turn, source],
                    send_sem=g_send.at[turn, 0], recv_sem=g_recv.at[turn, source],
                    device_id={"space": source}, device_id_type=MESH,
                ).wait_recv()
            total = gbuf[turn, 0]
            for source in range(1, sps):
                total = total + gbuf[turn, source]
            freq = held[0][0]
            for s in range(1, FCAP):
                freq = jnp.where(mine == s, held[s][0], freq)
            empty = freq == NF
            inverse = pack(inverse_factor(unpack(total * (1.0 / rows_total)), empty))
            pinv[turn] = inverse
            ibuf[turn, mine] = inverse
            copies = []
            for r in range(1, sps):
                peer = lax.rem(my + r, sps)
                copies.append(
                    pltpu.make_async_remote_copy(
                        src_ref=pinv.at[turn], dst_ref=ibuf.at[turn, mine],
                        send_sem=i_send.at[turn, r], recv_sem=i_recv.at[turn, mine],
                        device_id={"space": peer}, device_id_type=MESH,
                    )
                )
                copies[-1].start()
            for copy in copies:
                copy.wait_send()

        for s in range(FCAP):
            worker = first_worker + s

            @pl.when(my != worker)
            def _():
                pltpu.make_async_remote_copy(
                    src_ref=packed.at[turn, s], dst_ref=ibuf.at[turn, s],
                    send_sem=g_send.at[turn, s], recv_sem=i_recv.at[turn, s],
                    device_id={"space": worker}, device_id_type=MESH,
                ).wait()

            bd[s * nb : (s + 1) * nb, s * nb : (s + 1) * nb] = unpack(ibuf[turn, s])

    size = FCAP * nb
    across_hops[0].wait_recv()
    relays[0].start()
    for q in range(quarters):
        if q + 1 < quarters:
            across_hops[q + 1].wait_recv()
            relays[q + 1].start()
        sibling_hops[q].wait_recv()
        relays[q].wait_recv()
        xbuf[me] = near[q, 0]
        xbuf[sibling] = sib_in[q]
        for s in range(FCAP):
            freq, place = held[s]
            xbuf[across, s] = jnp.where(freq < NF, far_in[q][0, place], 0.0)
            xbuf[across_sibling, s] = jnp.where(freq < NF, far_in[q][1, place], 0.0)
        stacked = jnp.concatenate(
            [xbuf[:, s].reshape(nb, 2 * QP) for s in range(FCAP)], axis=0
        )
        x1, x2, x3 = split3(stacked)
        xs[q, 0], xs[q, 1], xs[q, 2] = x1, x2, x3
        p1 = mm_t(xs[q].reshape(3 * size, 2 * QP), x1)
        p2 = mm_t(xs[q, :2].reshape(2 * size, 2 * QP), x2)
        p3 = mm_t(x1, x3)
        gacc[...] += p1[:size] + (
            (p1[size : 2 * size] + p2[:size]) + ((p1[2 * size :] + p2[size:]) + p3)
        )
    reduce_and_factor(0)

    d1, d2, d3 = split3(bd[...])
    d321 = jnp.concatenate([d1, d2, d3], axis=0)
    gacc[...] = jnp.zeros(gacc.shape, F32)
    for q in range(quarters):
        p1 = mm(d321, xs[q, 0])
        p2 = mm(d321[: 2 * size], xs[q, 1])
        p3 = mm(d1, xs[q, 2])
        basis = p1[:size] + (
            (p1[size : 2 * size] + p2[:size]) + ((p1[2 * size :] + p2[size:]) + p3)
        )
        b1, b2 = split2(basis)
        bs[q, 0], bs[q, 1] = b1, b2
        p1 = mm_t(bs[q].reshape(2 * size, 2 * QP), b1)
        gacc[...] += p1[:size] + (p1[size:] + mm_t(b1, b2))
    reduce_and_factor(1)

    d1, d2 = split2(bd[...])
    d21 = jnp.concatenate([d1, d2], axis=0)
    tiles = quarters * QP // 128
    for q in range(quarters):
        p1 = mm(d21, bs[q, 0])
        modes = p1[:size] + (p1[size:] + mm(d1, bs[q, 1]))
        for c in range(2):
            for t in range(QP // 128):
                at = 2 * (q * (QP // 128) + t) + c
                lane = c * QP + t * 128
                out_ref[pl.ds(at, size, stride=2 * tiles), :] = modes[:, lane : lane + 128]
    for q in range(quarters):
        for copy in (across_hops[q], sibling_hops[q], relays[q]):
            copy.wait_send()


def hand_over(source, target, held, sem_in, sem_out):
    chunks = sem_in.shape[0]
    rows = source.shape[0] // chunks
    parts = [pl.ds(i * rows, rows) for i in range(chunks)]
    reads = [
        pltpu.make_async_copy(source.at[part], held.at[part], sem_in.at[i])
        for i, part in enumerate(parts)
    ]
    writes = [
        pltpu.make_async_copy(held.at[part], target.at[part], sem_out.at[i])
        for i, part in enumerate(parts)
    ]
    for read in reads:
        read.start()
    for read, write in zip(reads, writes):
        read.wait()
        write.start()
    for write in writes:
        write.wait()


def local(tms, sps, snapshots, block_starts, owner):
    samples, points = snapshots.shape
    blocks = block_starts.shape[0]
    nb = blocks * tms
    size = FCAP * nb
    quarters = points // QP
    tiles = points // 128
    table = jnp.asarray(dft_table())
    vm = pltpu.VMEM
    dma = pltpu.SemaphoreType.DMA
    modes = pl.pallas_call(
        functools.partial(kernel, tms, sps),
        out_shape=jax.ShapeDtypeStruct((size * tiles * 2, 128), F32),
        in_specs=[pl.BlockSpec(memory_space=pltpu.HBM)] * 4,
        out_specs=pl.BlockSpec(memory_space=pltpu.VMEM),
        scratch_shapes=[
            pltpu.SMEM((blocks,), jnp.int32),
            pltpu.SMEM((NF,), jnp.int32),
            vm((ROWS, NFFT), F32),
            vm((quarters, samples, QP), F32),
            vm((ROWS, blocks, samples), F32),
            vm((3 * ROWS * blocks, samples), BF16),
            vm((NF + 1, blocks, 2 * QP), F32),
            vm((quarters, 2, FCAP, blocks, 2 * QP), F32),
            vm((quarters, PAIR_CAP, blocks, 2 * QP), F32),
            vm((quarters, FCAP, blocks, 2 * QP), F32),
            vm((tms, FCAP, blocks, 2 * QP), F32),
            vm((quarters, 3, size, 2 * QP), BF16),
            vm((quarters, 2, size, 2 * QP), BF16),
            vm((size, size), F32),
            vm((2, FCAP, nb // 4, nb * 4), F32),
            vm((2, sps, nb // 4, nb * 4), F32),
            vm((2, nb // 4, nb * 4), F32),
            vm((2, FCAP, nb // 4, nb * 4), F32),
            vm((size, size), F32),
            dma((3,)),
            dma((quarters,)),
            dma((quarters, 3)),
            dma((quarters, 3)),
            dma((2, FCAP)),
            dma((2, sps)),
            dma((2, sps)),
            dma((2, FCAP)),
            *[vm((2, PAIR_CAP, blocks, 2 * QP), F32) for _ in range(quarters)],
        ],
        compiler_params=pltpu.CompilerParams(
            collective_id=0, has_side_effects=True, vmem_limit_bytes=VMEM_BYTES
        ),
    )(block_starts, owner, table, snapshots)
    modes = pl.pallas_call(
        hand_over,
        out_shape=jax.ShapeDtypeStruct(modes.shape, F32),
        in_specs=[pl.BlockSpec(memory_space=pltpu.HBM)],
        out_specs=pl.BlockSpec(memory_space=pltpu.HBM),
        scratch_shapes=[vm(modes.shape, F32), dma((FCAP,)), dma((FCAP,))],
        compiler_params=pltpu.CompilerParams(vmem_limit_bytes=VMEM_BYTES),
    )(modes)
    modes = modes.reshape(FCAP, nb, tiles, 2, 128).transpose(0, 1, 3, 2, 4)
    return modes.reshape(FCAP, nb, 2, points)


def solution(mesh):
    placed = (P("tm", "space"), P("tm"), P())
    return jax.shard_map(
        functools.partial(local, mesh.shape["tm"], mesh.shape["space"]),
        mesh=mesh, in_specs=placed, out_specs=P("tm", None, None, "space"), check_vma=False,
    )
```

```python
import functools

import jax
import jax.numpy as jnp
import numpy as np
from jax import lax
from jax.experimental import pallas as pl
from jax.experimental.pallas import tpu as pltpu
from jax.sharding import PartitionSpec as P

NFFT = 256
NF = 9
FCAP = 5
PAIR_CAP = 7
GAP = 112
VMEM_BYTES = 64 * 1024 * 1024 - 65536
ROWS = 2 * NF
QP = 256
F32 = jnp.float32
BF16 = jnp.bfloat16
MESH = pl.DeviceIdType.MESH


def dft_table():
    times = np.arange(NFFT)
    phase = (np.arange(NF)[:, None] * times[None, :]) % NFFT
    angle = 2.0 * np.pi / NFFT * phase
    window = 0.5 - 0.5 * np.cos(2.0 * np.pi / NFFT * times)
    table = np.stack([window * np.cos(angle), -window * np.sin(angle)], axis=1)
    return table.reshape(ROWS, NFFT).astype(np.float32)


def split3(x):
    a = x.astype(BF16)
    rest = x - a.astype(F32)
    b = rest.astype(BF16)
    c = (rest - b.astype(F32)).astype(BF16)
    return a, b, c


def split2(x):
    a = x.astype(BF16)
    return a, (x - a.astype(F32)).astype(BF16)


def mm(a, b):
    return jnp.dot(a, b, preferred_element_type=F32)


def mm_t(a, b):
    return lax.dot_general(a, b, (((1,), (1,)), ((), ())), preferred_element_type=F32)


def pack(square):
    n = square.shape[0] // 4
    return jnp.concatenate([square[n * i : n * i + n] for i in range(4)], axis=1)


def unpack(packed):
    n = packed.shape[1] // 4
    return jnp.concatenate([packed[:, n * i : n * i + n] for i in range(4)], axis=0)


def inverse_factor(gram, empty, panel=8):
    n = gram.shape[0]
    row = lax.broadcasted_iota(jnp.int32, (n, n), 0)
    col = lax.broadcasted_iota(jnp.int32, (n, n), 1)
    eye = jnp.where(row == col, 1.0, 0.0).astype(F32)
    gram = gram + jnp.where(empty, 1.0, 0.0) * eye
    work = jnp.concatenate([eye, gram, jnp.zeros((n, 128 - 2 * n), F32)], axis=1)
    done = []
    for first in range(0, n, panel):
        left = n - first
        rows = lax.broadcasted_iota(jnp.int32, (left, 128), 0)
        diag = jnp.ones((panel, 128), F32)
        cols = [
            jnp.broadcast_to(work[:, n + first + j : n + first + j + 1], (left, 128))
            for j in range(panel)
        ]
        for j in range(panel):
            pivot = cols[j][j : j + 1]
            diag = jnp.where(rows[:panel] == j, pivot, diag)
            factor = jnp.where(rows > j, cols[j] * (1.0 / pivot), 0.0)
            work = work - factor * work[j : j + 1]
            for i in range(j + 1, panel):
                cols[i] = cols[i] - factor * cols[i][j : j + 1]
        done.append(work[:panel] / jnp.sqrt(diag))
        work = work[panel:]
    return jnp.concatenate(done, axis=0)[:, :n]


def kernel(
    tms, sps, starts_hbm, owner_hbm, tab_hbm, snap_hbm, out_ref,
    starts_ref, owner_ref, tab_ref, snap, tallf, tall, spec, near, far, sib_in, xbuf,
    xs, bs, gacc, packed, gbuf, pinv, ibuf, bd,
    in_sem, snap_sem, a2a_send, a2a_recv, g_send, g_recv, i_send, i_recv, *far_in,
):
    quarters, samples = snap.shape[0], snap.shape[1]
    blocks = starts_hbm.shape[0]
    nb = blocks * tms
    rows_total = 2.0 * quarters * QP * sps
    me = lax.axis_index("tm")
    my = lax.axis_index("space")
    first_worker = sps // 4
    pair, half = me // 2, me % 2
    sibling = 2 * pair + (1 - half)
    across = 2 * (1 - pair) + half
    across_sibling = 2 * (1 - pair) + (1 - half)

    small = [
        pltpu.make_async_copy(source, target, in_sem.at[i])
        for i, (source, target) in enumerate(
            [(starts_hbm, starts_ref), (owner_hbm, owner_ref), (tab_hbm, tab_ref)]
        )
    ]
    for load in small:
        load.start()
    loads = [
        pltpu.make_async_copy(snap_hbm.at[:, pl.ds(q * QP, QP)], snap.at[q], snap_sem.at[q])
        for q in range(quarters)
    ]
    for load in loads:
        load.start()
    barrier = pltpu.get_barrier_semaphore()
    for peer in (sibling, across):
        pl.semaphore_signal(barrier, inc=1, device_id={"tm": peer}, device_id_type=MESH)
    for r in range(1, sps):
        pl.semaphore_signal(barrier, inc=1, device_id={"space": lax.rem(my + r, sps)}, device_id_type=MESH)
    tallf[...] = jnp.zeros(tallf.shape, F32)
    for load in small:
        load.wait()

    span = 2 * NFFT
    wide = jnp.concatenate([tab_ref[...], jnp.zeros((ROWS, span - NFFT), F32)], axis=1)
    for k in range(blocks):
        base = k * GAP // 128 * 128
        keep = min(span, samples - base)
        moved = pltpu.roll(wide, starts_ref[k] - me * samples - base, 1)
        tallf[:, k, base : base + keep] = moved[:, :keep]
    tall[...] = jnp.concatenate(split3(tallf[...].reshape(ROWS * blocks, samples)), axis=0)

    owners = [owner_ref[f] for f in range(NF)]
    owner_pair = [jnp.where(owners[f] >= 2, 1, 0) for f in range(NF)]
    rank, pair_rank = [], []
    for f in range(NF):
        rank.append(sum([jnp.where(owners[g] == owners[f], 1, 0) for g in range(f)], jnp.int32(0)))
        pair_rank.append(
            sum([jnp.where(owner_pair[g] == owner_pair[f], 1, 0) for g in range(f)], jnp.int32(0))
        )

    def owned(holder, s):
        freq, place = jnp.int32(NF), jnp.int32(0)
        for f in range(NF):
            hit = (owners[f] == holder) & (rank[f] == s)
            freq = jnp.where(hit, f, freq)
            place = jnp.where(hit, pair_rank[f], place)
        return freq, place

    held = [owned(me, s) for s in range(FCAP)]
    theirs = [owned(sibling, s)[0] for s in range(FCAP)]
    distant = []
    for place in range(PAIR_CAP):
        freq = jnp.int32(NF)
        for f in range(NF):
            freq = jnp.where((owner_pair[f] == 1 - pair) & (pair_rank[f] == place), f, freq)
        distant.append(freq)
    spec[NF] = jnp.zeros(spec.shape[1:], F32)
    gacc[...] = jnp.zeros(gacc.shape, F32)
    bd[...] = jnp.zeros(bd.shape, F32)

    def hop(source, target, kind, q, peer):
        return pltpu.make_async_remote_copy(
            src_ref=source, dst_ref=target,
            send_sem=a2a_send.at[q, kind], recv_sem=a2a_recv.at[q, kind],
            device_id={"tm": peer}, device_id_type=MESH,
        )

    across_hops = [hop(far.at[q], far_in[q].at[0], 0, q, across) for q in range(quarters)]
    sibling_hops = [hop(near.at[q, 1], sib_in.at[q], 1, q, sibling) for q in range(quarters)]
    relays = [hop(far_in[q].at[0], far_in[q].at[1], 2, q, sibling) for q in range(quarters)]
    m = ROWS * blocks
    for q in range(quarters):
        loads[q].wait()
        s1, s2, s3 = split3(snap[q])
        p1 = mm(tall[...], s1)
        p2 = mm(tall[: 2 * m], s2)
        p3 = mm(tall[:m], s3)
        spectrum = p1[:m] + ((p1[m : 2 * m] + p2[:m]) + ((p1[2 * m :] + p2[m:]) + p3))
        for f in range(NF):
            for c in range(2):
                at = (2 * f + c) * blocks
                spec[f, :, c * QP : (c + 1) * QP] = spectrum[at : at + blocks]
        for place in range(PAIR_CAP):
            far[q, place] = spec[distant[place]]
        if q == 0:
            pl.semaphore_wait(barrier, sps + 1)
        across_hops[q].start()
        for s in range(FCAP):
            near[q, 0, s] = spec[held[s][0]]
            near[q, 1, s] = spec[theirs[s]]
        sibling_hops[q].start()

    def reduce_and_factor(turn):
        for s in range(FCAP):
            sl = pl.ds(s * nb, nb)
            packed[turn, s] = pack(gacc[sl, sl])
        for s in range(FCAP):
            worker = first_worker + s

            @pl.when(my != worker)
            def _():
                pltpu.make_async_remote_copy(
                    src_ref=packed.at[turn, s], dst_ref=gbuf.at[turn, my],
                    send_sem=g_send.at[turn, s], recv_sem=g_recv.at[turn, my],
                    device_id={"space": worker}, device_id_type=MESH,
                ).start()

        @pl.when((my >= first_worker) & (my < first_worker + FCAP))
        def _():
            mine = my - first_worker
            gbuf[turn, my] = packed[turn, mine]
            for r in range(1, sps):
                source = lax.rem(my + r, sps)
                pltpu.make_async_remote_copy(
                    src_ref=packed.at[turn, 0], dst_ref=gbuf.at[turn, source],
                    send_sem=g_send.at[turn, 0], recv_sem=g_recv.at[turn, source],
                    device_id={"space": source}, device_id_type=MESH,
                ).wait_recv()
            total = gbuf[turn, 0]
            for source in range(1, sps):
                total = total + gbuf[turn, source]
            freq = held[0][0]
            for s in range(1, FCAP):
                freq = jnp.where(mine == s, held[s][0], freq)
            empty = freq == NF
            inverse = pack(inverse_factor(unpack(total * (1.0 / rows_total)), empty))
            pinv[turn] = inverse
            ibuf[turn, mine] = inverse
            copies = []
            for r in range(1, sps):
                peer = lax.rem(my + r, sps)
                copies.append(
                    pltpu.make_async_remote_copy(
                        src_ref=pinv.at[turn], dst_ref=ibuf.at[turn, mine],
                        send_sem=i_send.at[turn, r], recv_sem=i_recv.at[turn, mine],
                        device_id={"space": peer}, device_id_type=MESH,
                    )
                )
                copies[-1].start()
            for copy in copies:
                copy.wait_send()

        for s in range(FCAP):
            worker = first_worker + s

            @pl.when(my != worker)
            def _():
                pltpu.make_async_remote_copy(
                    src_ref=packed.at[turn, s], dst_ref=ibuf.at[turn, s],
                    send_sem=g_send.at[turn, s], recv_sem=i_recv.at[turn, s],
                    device_id={"space": worker}, device_id_type=MESH,
                ).wait()

            bd[s * nb : (s + 1) * nb, s * nb : (s + 1) * nb] = unpack(ibuf[turn, s])

    size = FCAP * nb
    across_hops[0].wait_recv()
    relays[0].start()
    for q in range(quarters):
        if q + 1 < quarters:
            across_hops[q + 1].wait_recv()
            relays[q + 1].start()
        sibling_hops[q].wait_recv()
        relays[q].wait_recv()
        xbuf[me] = near[q, 0]
        xbuf[sibling] = sib_in[q]
        for s in range(FCAP):
            freq, place = held[s]
            xbuf[across, s] = jnp.where(freq < NF, far_in[q][0, place], 0.0)
            xbuf[across_sibling, s] = jnp.where(freq < NF, far_in[q][1, place], 0.0)
        stacked = jnp.concatenate(
            [xbuf[:, s].reshape(nb, 2 * QP) for s in range(FCAP)], axis=0
        )
        x1, x2, x3 = split3(stacked)
        xs[q, 0], xs[q, 1], xs[q, 2] = x1, x2, x3
        p1 = mm_t(xs[q].reshape(3 * size, 2 * QP), x1)
        p2 = mm_t(xs[q, :2].reshape(2 * size, 2 * QP), x2)
        p3 = mm_t(x1, x3)
        gacc[...] += p1[:size] + (
            (p1[size : 2 * size] + p2[:size]) + ((p1[2 * size :] + p2[size:]) + p3)
        )
    reduce_and_factor(0)

    d1, d2, d3 = split3(bd[...])
    d321 = jnp.concatenate([d1, d2, d3], axis=0)
    gacc[...] = jnp.zeros(gacc.shape, F32)
    for q in range(quarters):
        p1 = mm(d321, xs[q, 0])
        p2 = mm(d321[: 2 * size], xs[q, 1])
        p3 = mm(d1, xs[q, 2])
        basis = p1[:size] + (
            (p1[size : 2 * size] + p2[:size]) + ((p1[2 * size :] + p2[size:]) + p3)
        )
        b1, b2 = split2(basis)
        bs[q, 0], bs[q, 1] = b1, b2
        p1 = mm_t(bs[q].reshape(2 * size, 2 * QP), b1)
        gacc[...] += p1[:size] + (p1[size:] + mm_t(b1, b2))
    reduce_and_factor(1)

    d1, d2 = split2(bd[...])
    d21 = jnp.concatenate([d1, d2], axis=0)
    tiles = quarters * QP // 128
    for q in range(quarters):
        p1 = mm(d21, bs[q, 0])
        modes = p1[:size] + (p1[size:] + mm(d1, bs[q, 1]))
        for c in range(2):
            for t in range(QP // 128):
                at = 2 * (q * (QP // 128) + t) + c
                lane = c * QP + t * 128
                out_ref[pl.ds(at, size, stride=2 * tiles), :] = modes[:, lane : lane + 128]
    for q in range(quarters):
        for copy in (across_hops[q], sibling_hops[q], relays[q]):
            copy.wait_send()


def hand_over(source, target, held, sem_in, sem_out):
    chunks = sem_in.shape[0]
    rows = source.shape[0] // chunks
    parts = [pl.ds(i * rows, rows) for i in range(chunks)]
    reads = [
        pltpu.make_async_copy(source.at[part], held.at[part], sem_in.at[i])
        for i, part in enumerate(parts)
    ]
    writes = [
        pltpu.make_async_copy(held.at[part], target.at[part], sem_out.at[i])
        for i, part in enumerate(parts)
    ]
    for read in reads:
        read.start()
    for read, write in zip(reads, writes):
        read.wait()
        write.start()
    for write in writes:
        write.wait()


def local(tms, sps, snapshots, block_starts, owner):
    samples, points = snapshots.shape
    blocks = block_starts.shape[0]
    nb = blocks * tms
    size = FCAP * nb
    quarters = points // QP
    tiles = points // 128
    table = jnp.asarray(dft_table())
    vm = pltpu.VMEM
    dma = pltpu.SemaphoreType.DMA
    modes = pl.pallas_call(
        functools.partial(kernel, tms, sps),
        out_shape=jax.ShapeDtypeStruct((size * tiles * 2, 128), F32),
        in_specs=[pl.BlockSpec(memory_space=pltpu.HBM)] * 4,
        out_specs=pl.BlockSpec(memory_space=pltpu.VMEM),
        scratch_shapes=[
            pltpu.SMEM((blocks,), jnp.int32),
            pltpu.SMEM((NF,), jnp.int32),
            vm((ROWS, NFFT), F32),
            vm((quarters, samples, QP), F32),
            vm((ROWS, blocks, samples), F32),
            vm((3 * ROWS * blocks, samples), BF16),
            vm((NF + 1, blocks, 2 * QP), F32),
            vm((quarters, 2, FCAP, blocks, 2 * QP), F32),
            vm((quarters, PAIR_CAP, blocks, 2 * QP), F32),
            vm((quarters, FCAP, blocks, 2 * QP), F32),
            vm((tms, FCAP, blocks, 2 * QP), F32),
            vm((quarters, 3, size, 2 * QP), BF16),
            vm((quarters, 2, size, 2 * QP), BF16),
            vm((size, size), F32),
            vm((2, FCAP, nb // 4, nb * 4), F32),
            vm((2, sps, nb // 4, nb * 4), F32),
            vm((2, nb // 4, nb * 4), F32),
            vm((2, FCAP, nb // 4, nb * 4), F32),
            vm((size, size), F32),
            dma((3,)),
            dma((quarters,)),
            dma((quarters, 3)),
            dma((quarters, 3)),
            dma((2, FCAP)),
            dma((2, sps)),
            dma((2, sps)),
            dma((2, FCAP)),
            *[vm((2, PAIR_CAP, blocks, 2 * QP), F32) for _ in range(quarters)],
        ],
        compiler_params=pltpu.CompilerParams(
            collective_id=0, has_side_effects=True, vmem_limit_bytes=VMEM_BYTES
        ),
    )(block_starts, owner, table, snapshots)
    modes = pl.pallas_call(
        hand_over,
        out_shape=jax.ShapeDtypeStruct(modes.shape, F32),
        in_specs=[pl.BlockSpec(memory_space=pltpu.HBM)],
        out_specs=pl.BlockSpec(memory_space=pltpu.HBM),
        scratch_shapes=[vm(modes.shape, F32), dma((FCAP,)), dma((FCAP,))],
        compiler_params=pltpu.CompilerParams(vmem_limit_bytes=VMEM_BYTES),
    )(modes)
    modes = modes.reshape(FCAP, nb, tiles, 2, 128).transpose(0, 1, 3, 2, 4)
    return modes.reshape(FCAP, nb, 2, points)


def solution(mesh):
    placed = (P("tm", "space"), P("tm"), P())
    return jax.shard_map(
        functools.partial(local, mesh.shape["tm"], mesh.shape["space"]),
        mesh=mesh, in_specs=placed, out_specs=P("tm", None, None, "space"), check_vma=False,
    )
```
